32 devices in a mesh: seq: 8 (over z, y), fsdp: 4 (over x, core).
Axes of the slice: x: 2, y: 2, z: 4, core: 2. Of those that a mesh axis runs over, the one named last changes fastest.
Arguments:
- queries: bfloat16 [4, 1024, 2048], P('fsdp', 'seq'), may hold values from -160 to 160
- key_rows: bfloat16 [4, 1024, 2048], P('fsdp', 'seq'), may hold values from -4.5 to 4.5
- value_rows: bfloat16 [4, 1024, 2048], P('fsdp', 'seq'), may hold values from -6 to 6
- out_grad: bfloat16 [4, 1024, 2048], P('fsdp', 'seq'), may hold values from -6 to 6
- inputs: bfloat16 [4, 1024, 4096], P('fsdp', 'seq'), may hold values from -6 to 6
- router_weight: bfloat16 [4096], P('fsdp'), may hold values from -0.09375 to 0.09375
- counts: int32 [4, 8], P('fsdp', 'seq'), may hold values from 0 to 128, as said below
- picked_pos: int32 [4, 1024], P('fsdp', 'seq'), may hold values from -1 to 511, as said below
Outputs:
- grad_queries: bfloat16 [4, 1024, 2048], P('fsdp', 'seq')
- grad_keys: bfloat16 [4, 1024, 2048], P('fsdp', 'seq')
- grad_values: bfloat16 [4, 1024, 2048], P('fsdp', 'seq')
- grad_router: float32 [4096], P(('seq', 'fsdp'))
The draws below stay inside these ranges and needn't reach their ends.
Inputs may be any that keep to these rules, and one draw needn't show every extreme that they name: `counts`: devices 2i and 2i + 1 of a sequence together hold 128 picked tokens; some device of every sequence holds 128 and its partner none. `picked_pos`: the first counts slots of a device hold the local positions of its picked tokens in increasing order, the other slots -1.
All inputs are finite; a program needn't handle non-finite values.
Results may differ from the reference program's by a relative error of at most 0.015.
Values may be sent and summed in bfloat16 or wider, within the bound.
No kernel may reach another device: no remote copies, remote signals or barrier semaphores. Data moves between devices by JAX's collectives and lax.ppermute only.
A program may use at most 128 MiB of HBM per device.

```python
import jax
import jax.numpy as jnp
from jax import lax

D = 4096
HEADS = 16
HEAD_DIM = 128
TOK_DEV = 512
PICK = 64
CAP = 128
PICKED = 512
N_SEQ = 8
N_FSDP = 4


def key_base(key):
    shape_all = (N_FSDP, N_SEQ * CAP, HEADS * HEAD_DIM)
    return jnp.clip(jax.random.normal(key, shape_all, jnp.float32), -4.5, 4.5)


def pair_counts(key):
    key = jax.random.fold_in(key, 11)
    key_one, key_two, key_three = jax.random.split(key, 3)
    half_seq = N_SEQ // 2
    moved = jax.random.randint(key_one, (N_FSDP, half_seq), -PICK, PICK + 1)
    target = jax.random.randint(key_two, (N_FSDP, 1), 0, half_seq)
    flipped = jax.random.randint(key_three, (N_FSDP, 1), 0, 2) * 2 - 1
    moved = jnp.where(jnp.arange(half_seq)[None, :] == target, flipped * PICK, moved)
    paired = jnp.stack([PICK + moved, PICK - moved], axis=-1)
    return paired.reshape(N_FSDP, N_SEQ).astype(jnp.int32)


def draw_counts(key, part):
    result = pair_counts(key)
    return result


def draw_picked_pos(key, part):
    held = pair_counts(key)
    key = jax.random.fold_in(key, 5)
    local_pos = jnp.arange(TOK_DEV, dtype=jnp.int32)
    scores_int = jax.random.randint(key, (N_FSDP, N_SEQ, TOK_DEV), 0, 1 << 18) * TOK_DEV + local_pos
    ranking = jnp.argsort(jnp.argsort(scores_int, axis=-1), axis=-1)
    chosen = ranking < held[..., None]
    ordered = jnp.argsort(jnp.where(chosen, local_pos, local_pos + TOK_DEV), axis=-1)[..., :CAP]
    slot_ids = jnp.arange(CAP, dtype=jnp.int32)
    result = jnp.where(slot_ids < held[..., None], ordered, -1)
    return result.reshape(N_FSDP, N_SEQ * CAP).astype(jnp.int32)


def draw_key_rows(key, part):
    base = key_base(key)
    return base.astype(jnp.bfloat16)


def draw_queries(key, part):
    key = jax.random.fold_in(key, 4)
    key_one = jax.random.fold_in(key, 0)
    shape_all = (N_FSDP, N_SEQ * CAP, HEADS * HEAD_DIM)
    fresh = jnp.clip(jax.random.normal(key_one, shape_all, jnp.float32), -4.5, 4.5)
    return fresh.astype(jnp.bfloat16)


def spiked(array, own_key, source, target, blocks, factor):
    def block_of(position):
        return (jnp.arange(array.shape[position]) // (array.shape[position] // blocks)).reshape((-1,) + (1,) * (array.ndim - 1 - position))

    near = jax.random.permutation(own_key, blocks)[block_of(target)]
    other_side = (block_of(target) + blocks // 2) % blocks
    return jnp.where((block_of(source) == near) | (block_of(source) == other_side), factor * array, array)


def block_levels(own_key, shape, shards, low, largest):
    level = 1.0
    for dim, parts in shards:
        heights = jax.random.uniform(jax.random.fold_in(jax.random.fold_in(own_key, 6), dim), (parts,), jnp.float32, low / len(shards), largest / len(shards))
        level = level * jnp.repeat(jnp.exp(heights), shape[dim] // parts).reshape((-1,) + (1,) * (len(shape) - 1 - dim))
    return level


def scatter_about(rng, shape, spread, bound, cuts=(), kind=jnp.bfloat16):
    loudness = block_levels(rng, shape, cuts, -0.22, 0.18) if cuts else 1.0
    array = jax.random.normal(rng, shape, jnp.float32) * spread * loudness
    return jnp.minimum(jnp.maximum(array, -bound), bound).astype(kind)


def gaussian_with(stream_key, dims, deviation, limit, shards, heavy, kind=jnp.bfloat16):
    drawn = deviation * jax.random.normal(stream_key, dims, jnp.float32)
    if shards:
        drawn = drawn * block_levels(stream_key, dims, shards, -0.22, 0.18)
    return jnp.clip(spiked(drawn, jax.random.fold_in(stream_key, 3), *heavy), -limit, limit).astype(kind)


def setup_inputs(seed: int = 0) -> dict:
    arg_keys = jax.random.split(jax.random.key(seed), 9)
    return {
        "queries": draw_queries(jax.random.fold_in(arg_keys[8], 71), 0),
        "key_rows": draw_key_rows(jax.random.fold_in(arg_keys[8], 71), 0),
        "value_rows": scatter_about(arg_keys[2], (N_FSDP, N_SEQ * CAP, HEADS * HEAD_DIM), 1.0, 6.0, ((0, 4), (1, 8))),
        "out_grad": scatter_about(arg_keys[3], (N_FSDP, N_SEQ * CAP, HEADS * HEAD_DIM), 1.0, 6.0, ((0, 4), (1, 8))),
        "inputs": gaussian_with(arg_keys[4], (N_FSDP, N_SEQ * CAP, D), 1.0, 6.0, ((0, 4), (1, 8)), (1, 2, 8, 2.0)),
        "router_weight": scatter_about(arg_keys[5], (D,), D ** -0.5, 0.09375, ((0, 4),)),
        "counts": draw_counts(jax.random.fold_in(arg_keys[8], 71), 0),
        "picked_pos": draw_picked_pos(jax.random.fold_in(arg_keys[8], 71), 0),
    }


THETA = 500000.0
NEG = -1e30


def angle_table(positions):
    half_dim = HEAD_DIM // 2
    inverse_freq = THETA ** (-(jnp.arange(half_dim, dtype=jnp.float32) * 2.0 / HEAD_DIM))
    angles = positions.astype(jnp.float32)[:, None] * inverse_freq[None, :]
    return jnp.cos(angles), jnp.sin(angles)


def rotate(vectors, cosine, sine, direction):
    row_count = vectors.shape[0]
    parted = vectors.reshape(row_count, HEADS, HEAD_DIM)
    half_dim = HEAD_DIM // 2
    lower_half = parted[:, :, :half_dim]
    upper_half = parted[:, :, half_dim:]
    cos_b = cosine[:, None, :]
    sin_b = direction * sine[:, None, :]
    joined = jnp.concatenate([lower_half * cos_b - upper_half * sin_b, upper_half * cos_b + lower_half * sin_b], axis=2)
    return joined.reshape(row_count, HEADS * HEAD_DIM)


def one_sequence(router_weight, query_all, key_all, value_all, grad_all, input_all, count_row, pos_row):
    slots = N_SEQ * CAP
    width = HEADS * HEAD_DIM
    score_scale = HEAD_DIM ** -0.5
    slot_ids = jnp.arange(slots, dtype=jnp.int32)
    owner_dev = slot_ids // CAP
    is_valid = (slot_ids % CAP) < count_row[owner_dev]
    row_order = jnp.argsort(jnp.where(is_valid, slot_ids, slot_ids + slots))[:PICKED].astype(jnp.int32)
    positions = (owner_dev * TOK_DEV + pos_row)[row_order]
    gate_all = jax.nn.sigmoid(jnp.dot(input_all, router_weight, preferred_element_type=jnp.float32))
    gate = gate_all[row_order]
    cosine, sine = angle_table(positions)
    query_rot = rotate(query_all[row_order].astype(jnp.float32), cosine, sine, 1.0).astype(jnp.bfloat16)
    key_rot = rotate(key_all[row_order].astype(jnp.float32), cosine, sine, 1.0).astype(jnp.bfloat16)
    grad_scaled = (gate[:, None] * grad_all[row_order].astype(jnp.float32)).astype(jnp.bfloat16)
    query_heads = query_rot.astype(jnp.float32).reshape(PICKED, HEADS, HEAD_DIM)
    key_heads = key_rot.astype(jnp.float32).reshape(PICKED, HEADS, HEAD_DIM)
    value_heads = value_all[row_order].astype(jnp.float32).reshape(PICKED, HEADS, HEAD_DIM)
    grad_heads = grad_scaled.astype(jnp.float32).reshape(PICKED, HEADS, HEAD_DIM)
    causal = (jnp.arange(PICKED)[:, None] >= jnp.arange(PICKED)[None, :])[None]
    scores = jnp.einsum("qhd,khd->hqk", query_heads, key_heads) * score_scale
    scores = jnp.where(causal, scores, NEG)
    row_top = jnp.max(scores, axis=-1)
    expo = jnp.where(causal, jnp.exp(scores - row_top[..., None]), 0.0)
    row_sum = jnp.sum(expo, axis=-1)
    log_total = row_top + jnp.log(row_sum)
    rounded = expo.astype(jnp.bfloat16).astype(jnp.float32)
    attended = jnp.einsum("hqk,khd->hqd", rounded, value_heads) / row_sum[..., None]
    delta = jnp.sum(grad_heads.transpose(1, 0, 2) * attended, axis=-1)
    weights_bf = jnp.where(causal, jnp.exp(scores - log_total[..., None]), 0.0).astype(jnp.bfloat16).astype(jnp.float32)
    grad_probs = jnp.einsum("qhd,khd->hqk", grad_heads, value_heads)
    grad_scores = (score_scale * weights_bf * (grad_probs - delta[..., None])).astype(jnp.bfloat16).astype(jnp.float32)
    grad_qrot = jnp.einsum("hqk,khd->qhd", grad_scores, key_heads).reshape(PICKED, width)
    grad_krot = jnp.einsum("hqk,qhd->khd", grad_scores, query_heads).reshape(PICKED, width)
    grad_vals = jnp.einsum("hqk,qhd->khd", weights_bf, grad_heads).reshape(PICKED, width)
    grad_q = rotate(grad_qrot, cosine, sine, -1.0).astype(jnp.bfloat16)
    grad_k = rotate(grad_krot, cosine, sine, -1.0).astype(jnp.bfloat16)
    grad_v = grad_vals.astype(jnp.bfloat16)
    router_term = (1.0 - gate) * jnp.sum(delta, axis=0)
    grad_w = jnp.dot(router_term, input_all[row_order].astype(jnp.float32), precision=lax.Precision.HIGHEST)
    empty = jnp.zeros((slots, width), jnp.bfloat16)
    return empty.at[row_order].set(grad_q), empty.at[row_order].set(grad_k), empty.at[row_order].set(grad_v), grad_w


def reference(queries, key_rows, value_rows, out_grad, inputs, router_weight, counts, picked_pos):
    def per_sequence(packed):
        return one_sequence(router_weight, *packed)

    grad_q, grad_k, grad_v, grad_w = lax.map(per_sequence, (queries, key_rows, value_rows, out_grad, inputs, counts, picked_pos))
    return grad_q, grad_k, grad_v, jnp.sum(grad_w, axis=0)
```

```python
import functools

import jax
import jax.numpy as jnp
import numpy as np
from jax import lax
from jax.experimental import pallas as pl
from jax.experimental.pallas import tpu as pltpu
from jax.sharding import PartitionSpec as P

HEADS = 16
HEAD_DIM = 128
HALF_DIM = HEAD_DIM // 2
TOK_DEV = 512
THETA = 500000.0
NEG = -1e30
SCALE = HEAD_DIM ** -0.5
BF16 = jnp.bfloat16
F32 = jnp.float32
PARAMS = pltpu.CompilerParams(vmem_limit_bytes=40 * 1024 * 1024)
VMEM = pl.BlockSpec(memory_space=pltpu.VMEM)
SMEM = pl.BlockSpec(memory_space=pltpu.SMEM)


def swapped(array, apart):
    return lax.ppermute(array, "seq", [(i, i ^ apart) for i in range(lax.axis_size("seq"))])


def dot(a, b, contract):
    return lax.dot_general(a, b, ((contract[0], contract[1]), ((), ())), preferred_element_type=F32)


def pack_matrices(place, cap):
    parity, first = place[0], place[2]
    row = lax.broadcasted_iota(jnp.int32, (cap, cap), 0)
    slot = lax.broadcasted_iota(jnp.int32, (cap, cap), 1)
    even = jnp.where((row == slot) & (row < first), 1.0, 0.0)
    odd = jnp.where((row == slot + first) & (row >= first), 1.0, 0.0)
    is_even = parity == 0
    own = jnp.where(is_even, even, odd).astype(BF16)
    other = jnp.where(is_even, odd, even).astype(BF16)
    return own, other


def rolled(vectors):
    return pltpu.roll(vectors, HALF_DIM, 1)


def pack_kernel(groups, chunk, place, freq_ref, note_own, note_in, *refs):
    if chunk == 0:
        q_ref, k_ref, v_ref, g_ref, in_ref, *outs, table_ref = refs
    else:
        q_ref, k_ref, v_ref, g_ref, in_ref, table_ref, *outs = refs
    cap = q_ref.shape[0]
    group, first = place[1], place[2]
    own_hot, in_hot = pack_matrices(place, cap)
    row = lax.broadcasted_iota(jnp.int32, (cap, HEAD_DIM), 0)
    lane = lax.broadcasted_iota(jnp.int32, (cap, HEAD_DIM), 1)
    if chunk == 0:
        is_even = place[0] == 0
        note_a = jnp.where(is_even, note_own[...], note_in[...])
        note_b = jnp.where(is_even, note_in[...], note_own[...])
        note = jnp.where(row < first, note_a, pltpu.roll(note_b, first, 0))
        turned = rolled(note)
        position = jnp.where(lane < HALF_DIM, note, turned)
        gate = jnp.where(lane < HALF_DIM, turned, note)
        angle = position * freq_ref[0:1, :]
        cosine = jnp.cos(angle)
        sine = jnp.where(lane < HALF_DIM, -1.0, 1.0) * jnp.sin(angle)
        table_ref[0] = cosine
        table_ref[1] = sine
        table_ref[2] = gate
    else:
        cosine, sine, gate = table_ref[0], table_ref[1], table_ref[2]

    for m in range(groups):
        columns = pl.ds(pl.multiple_of((group ^ m) * HEAD_DIM, HEAD_DIM), HEAD_DIM)
        for t, ref in enumerate((q_ref, k_ref, v_ref, g_ref)):
            rows = dot(own_hot, ref[:, columns], ((1,), (0,)))
            rows += dot(in_hot, in_ref[t, :, columns], ((1,), (0,)))
            if t < 2:
                rows = rows * cosine + rolled(rows) * sine
            elif t == 3:
                rows = rows * gate
            outs[m][t] = rows.astype(BF16)


def attention_kernel(groups, place, *refs):
    ins, outs, delta_ref, rows_ref, dk_ref, dv_ref = (
        refs[:groups], refs[groups:2 * groups], refs[2 * groups], refs[2 * groups + 1], refs[2 * groups + 2],
        refs[2 * groups + 3],
    )
    cap = ins[0].shape[1]
    group = place[1]
    for m in range(groups):
        start = pl.multiple_of((group ^ m) * cap, cap)
        for t in range(4):
            rows_ref[t, pl.ds(start, cap), :] = ins[m][t]
    dk_ref[...] = jnp.zeros_like(dk_ref)
    dv_ref[...] = jnp.zeros_like(dv_ref)
    key = lax.broadcasted_iota(jnp.int32, (cap, cap), 0)
    query = lax.broadcasted_iota(jnp.int32, (cap, cap), 1)
    kept = query >= key
    for i in range(groups):
        here = pl.ds(i * cap, cap)
        q, g = rows_ref[0, here, :], rows_ref[3, here, :]
        upto = (i + 1) * cap
        k, v = rows_ref[1, :upto, :], rows_ref[2, :upto, :]
        s = dot(k, q, ((1,), (1,))) * SCALE
        last = jnp.where(kept, s[i * cap:], NEG)
        s = last if i == 0 else jnp.concatenate([s[:i * cap], last], axis=0)
        top = jnp.max(s, axis=0, keepdims=True)
        e = jnp.exp(s - top)
        p = e * (1.0 / jnp.sum(e, axis=0, keepdims=True))
        dp = dot(v, g, ((1,), (1,)))
        delta = jnp.sum(p * dp, axis=0, keepdims=True)
        delta_ref[:, i * cap:upto] = jnp.broadcast_to(delta, (8, cap))
        p16 = p.astype(BF16)
        ds = (p16.astype(F32) * (dp - delta) * SCALE).astype(BF16)
        dv_ref[:upto, :] += dot(p16, g, ((1,), (0,)))
        dk_ref[:upto, :] += dot(ds, q, ((1,), (0,)))
        rows_ref[0, here, :] = dot(ds, k, ((0,), (0,))).astype(BF16)
    for m in range(groups):
        block = pl.ds(pl.multiple_of((group ^ m) * cap, cap), cap)
        outs[m][0] = rows_ref[0, block, :]
        outs[m][1] = dk_ref[block, :].astype(BF16)
        outs[m][2] = dv_ref[block, :].astype(BF16)


def unpack_kernel(groups, place, table_ref, *refs):
    ins, own_ref, send_ref = refs[:groups], refs[groups], refs[groups + 1]
    cap = ins[0].shape[1]
    group = place[1]
    own_hot, in_hot = pack_matrices(place, cap)
    cosine, sine = table_ref[0], table_ref[1]
    for m in range(groups):
        columns = pl.ds(pl.multiple_of((group ^ m) * HEAD_DIM, HEAD_DIM), HEAD_DIM)
        for t in range(3):
            rows = ins[m][t]
            if t < 2:
                rows = rows.astype(F32)
                rows = (rows * cosine - rolled(rows) * sine).astype(BF16)
            own_ref[t, :, columns] = dot(own_hot, rows, ((0,), (0,))).astype(BF16)
            send_ref[t, :, columns] = dot(in_hot, rows, ((0,), (0,))).astype(BF16)


def place_kernel(chunks, place, *refs):
    owns, others, outs = refs[:chunks], refs[chunks:2 * chunks], refs[2 * chunks:]
    parity = place[0]
    wide = owns[0].shape[2]
    for c in range(chunks):
        own = pl.ds(pl.multiple_of((parity * chunks + c) * wide, wide), wide)
        other = pl.ds(pl.multiple_of(((1 - parity) * chunks + c) * wide, wide), wide)
        for t in range(3):
            outs[t][:, own] = owns[c][t]
            outs[t][:, other] = others[c][t]


def per_device(queries, key_rows, value_rows, out_grad, inputs, router_weight, counts, picked_pos):
    arrays = (queries[0], key_rows[0], value_rows[0], out_grad[0])
    input_own = inputs[0]
    own_count = counts[0, 0]
    cap, width = arrays[0].shape
    seq_size = lax.axis_size("seq")
    groups = seq_size // 2
    chunks = HEADS // seq_size
    wide = groups * HEAD_DIM
    seq_index = lax.axis_index("seq")
    parity, group = seq_index % 2, seq_index // 2
    first = jnp.where(parity == 0, own_count, cap - own_count)
    place = jnp.stack([parity, group, first]).astype(jnp.int32)

    arrived = []
    for c in range(chunks):
        begin = ((1 - parity) * chunks + c) * wide
        arrived.append(swapped(jnp.stack([lax.dynamic_slice_in_dim(a, begin, wide, 1) for a in arrays]), 1))

    router_full = lax.all_gather(router_weight, "fsdp", axis=0, tiled=True)
    gate = jax.nn.sigmoid(jnp.dot(input_own, router_full, preferred_element_type=F32))
    position = (seq_index * TOK_DEV + picked_pos[0]).astype(F32)
    note = jnp.where(jnp.arange(HEAD_DIM)[None, :] < HALF_DIM, position[:, None], gate[:, None])
    note_in = swapped(note, 1)

    power = THETA ** (-(np.arange(HALF_DIM) * 2.0 / HEAD_DIM))
    freq = jnp.asarray(np.broadcast_to(np.tile(power, 2).astype(np.float32), (8, HEAD_DIM)))

    piece = jax.ShapeDtypeStruct((4, cap, HEAD_DIM), BF16)
    table = None
    grads, deltas = [], []
    for c in range(chunks):
        block = pl.BlockSpec((cap, wide), lambda i, at, c=c: (0, at[0] * chunks + c))
        outs = pl.pallas_call(
            functools.partial(pack_kernel, groups, c),
            grid_spec=pltpu.PrefetchScalarGridSpec(
                num_scalar_prefetch=1,
                grid=(1,),
                in_specs=[VMEM] * 3 + [block] * 4 + [VMEM] + ([] if c == 0 else [VMEM]),
                out_specs=[VMEM] * (groups + (1 if c == 0 else 0)),
            ),
            out_shape=[piece] * groups + ([jax.ShapeDtypeStruct((3, cap, HEAD_DIM), F32)] if c == 0 else []),
            compiler_params=PARAMS,
            name=f"pack_{c}",
        )(place, freq, note, note_in, *arrays, arrived[c], *([] if c == 0 else [table]))
        if c == 0:
            table = outs[groups]
        pieces = [outs[0]] + [swapped(outs[m], 2 * m) for m in range(1, groups)]
        total = groups * cap
        outs = pl.pallas_call(
            functools.partial(attention_kernel, groups),
            in_specs=[SMEM] + [VMEM] * groups,
            out_specs=[VMEM] * (groups + 1),
            out_shape=[jax.ShapeDtypeStruct((3, cap, HEAD_DIM), BF16)] * groups
            + [jax.ShapeDtypeStruct((8, total), F32)],
            scratch_shapes=[
                pltpu.VMEM((4, total, HEAD_DIM), BF16),
                pltpu.VMEM((total, HEAD_DIM), F32),
                pltpu.VMEM((total, HEAD_DIM), F32),
            ],
            compiler_params=PARAMS,
            name=f"attention_{c}",
        )(place, *pieces)
        grads.append(outs[:groups])
        deltas.append(outs[groups][0])

    owns, others = [], []
    for c in range(chunks):
        pieces = [grads[c][0]] + [swapped(grads[c][m], 2 * m) for m in range(1, groups)]
        slots = jax.ShapeDtypeStruct((3, cap, wide), BF16)
        own, send = pl.pallas_call(
            functools.partial(unpack_kernel, groups),
            in_specs=[SMEM] + [VMEM] * (groups + 1),
            out_specs=[VMEM] * 2,
            out_shape=[slots] * 2,
            compiler_params=PARAMS,
            name=f"unpack_{c}",
        )(place, table, *pieces)
        owns.append(own)
        others.append(swapped(send, 1))
    grad_q, grad_k, grad_v = pl.pallas_call(
        functools.partial(place_kernel, chunks),
        in_specs=[SMEM] + [VMEM] * (2 * chunks),
        out_specs=[VMEM] * 3,
        out_shape=[jax.ShapeDtypeStruct((cap, width), BF16)] * 3,
        compiler_params=PARAMS,
        name="place",
    )(place, *owns, *others)

    delta = functools.reduce(jnp.add, deltas).reshape(groups, 1, cap)
    to_pair = jnp.broadcast_to(delta, (groups, 2, cap)).reshape(seq_size, cap)
    delta = jnp.sum(lax.all_to_all(to_pair, "seq", 0, 0), axis=0)
    slot = jnp.arange(cap)
    is_valid = slot < own_count
    start = jnp.where(parity == 0, 0, first)
    padded = jnp.concatenate([delta, jnp.zeros_like(delta)])
    own_delta = lax.dynamic_slice_in_dim(padded, start, cap, 0)
    router_term = jnp.where(is_valid, (1.0 - gate) * own_delta, 0.0)
    partial_value = jnp.dot(router_term, input_own.astype(F32), precision=lax.Precision.HIGHEST)
    devices = seq_size * lax.axis_size("fsdp")
    shares = lax.all_to_all(partial_value.reshape(devices, -1), ("seq", "fsdp"), 0, 0)
    grad_router = jnp.sum(shares, axis=0)
    return grad_q[None], grad_k[None], grad_v[None], grad_router


def solution(mesh):
    rows = P("fsdp", "seq", None)
    placed = (rows, rows, rows, rows, rows, P("fsdp"), P("fsdp", "seq"), P("fsdp", "seq"))
    return jax.shard_map(
        per_device,
        mesh=mesh,
        in_specs=placed,
        out_specs=(rows, rows, rows, P(("seq", "fsdp"))),
        check_vma=False,
    )
```

```python
import functools
import math

import jax
import jax.numpy as jnp
from jax import lax
from jax.experimental import pallas as pl
from jax.experimental.pallas import tpu as pltpu
from jax.sharding import PartitionSpec as P

HEADS = 16
HEAD_DIM = 128
HALF_DIM = HEAD_DIM // 2
TOK_DEV = 512
THETA = 500000.0
NEG = -1e30
SCALE = HEAD_DIM ** -0.5
BF16 = jnp.bfloat16
F32 = jnp.float32
PARAMS = pltpu.CompilerParams(vmem_limit_bytes=40 * 1024 * 1024)
FRONT = 63
SMALL = pl.CostEstimate(flops=1 << 20, bytes_accessed=1 << 16, transcendentals=0)
LARGE = pl.CostEstimate(flops=1 << 28, bytes_accessed=1 << 16, transcendentals=0)
VMEM = pl.BlockSpec(memory_space=pltpu.VMEM)
ANY = pl.BlockSpec(memory_space=pl.ANY)
SMEM = pl.BlockSpec(memory_space=pltpu.SMEM)


def swapped(array):
    return lax.ppermute(array, "seq", [(i, i ^ 1) for i in range(lax.axis_size("seq"))])


def spread(pieces):
    size = lax.axis_size("seq")
    arrived = [
        lax.ppermute(pieces[m], "seq", [(i, i ^ (2 * m)) for i in range(size)]) for m in range(len(pieces) - 1, 0, -1)
    ]
    return arrived + [pieces[0]]


def after(value, *done):
    return lax.optimization_barrier((value, *done))[0]


def call(kernel, name, shapes, *operands, scratch_shapes=(), cost_estimate=SMALL):
    return pl.pallas_call(
        kernel,
        in_specs=[SMEM if a.shape == (1, 1) else VMEM for a in operands],
        out_specs=[VMEM] * len(shapes),
        out_shape=[jax.ShapeDtypeStruct(shape, dtype) for shape, dtype in shapes],
        scratch_shapes=scratch_shapes,
        compiler_params=PARAMS,
        cost_estimate=cost_estimate,
        name=name,
    )(*operands)


def dot(a, b, contract):
    return lax.dot_general(a, b, ((contract[0], contract[1]), ((), ())), preferred_element_type=F32)


def lanes(index, width=HEAD_DIM):
    if isinstance(index, int):
        return slice(index * width, (index + 1) * width)
    return pl.ds(pl.multiple_of(index * width, HEAD_DIM), width)


def grid_of(cap):
    row = lax.broadcasted_iota(jnp.int32, (cap, cap), 0)
    column = lax.broadcasted_iota(jnp.int32, (cap, cap), 1)
    return row, column


def own_place(counts):
    index = lax.axis_index("seq")
    return index & 1, index >> 1, counts[0, 0]


def places(counts, cap):
    parity, _, count = own_place(counts)
    first = jnp.where(parity == 0, count, cap - count)
    row, slot = grid_of(cap)
    even = jnp.where((row == slot) & (row < first), 1.0, 0.0)
    odd = jnp.where((row == slot + first) & (row >= first), 1.0, 0.0)
    is_even = parity == 0
    return jnp.where(is_even, even, odd).astype(BF16), jnp.where(is_even, odd, even).astype(BF16)


def rotated(rows, table_ref, direction):
    rows = rows.astype(F32)
    turned = pltpu.roll(rows, HALF_DIM, 1) * table_ref[1]
    rows = rows * table_ref[0]
    return (rows + turned if direction > 0 else rows - turned).astype(BF16)


def put(hot, rows):
    return dot(hot, rows, ((1,), (0,))).astype(BF16)


def taken(hot, rows):
    return dot(hot, rows, ((0,), (0,))).astype(BF16)


def front_kernel(groups, counts, pos_ref, v_ref, k_ref, q_ref, *refs):
    outs, (out_ref, table_ref, v_buffer, kq_buffer, sems) = refs[:groups], refs[groups:]
    cap, half = out_ref.shape[1:]
    wide = outs[0].shape[2]
    heads = half // HEAD_DIM
    parity, group, _ = own_place(counts)
    copies = [pltpu.make_async_copy(v_ref, v_buffer, sems.at[0])]
    for t, ref in enumerate((k_ref, q_ref)):
        copies.append(pltpu.make_async_copy(ref.at[:, lanes(1 - parity, half)], kq_buffer.at[t], sems.at[1 + t]))
    for copy in copies:
        copy.start()
    own_hot, _ = places(counts, cap)
    row, column = grid_of(cap)
    position = (lax.axis_index("seq") * TOK_DEV + pos_ref[0:1, :]).astype(F32)
    position = jnp.sum(jnp.where(row == column, position, 0.0), axis=1, keepdims=True)
    lane = lax.broadcasted_iota(jnp.int32, (cap, HEAD_DIM), 1)
    feature = jnp.where(lane < HALF_DIM, lane, lane - HALF_DIM).astype(F32)
    angle = position * jnp.exp(feature * (-2.0 / HEAD_DIM * math.log(THETA)))
    table_ref[0] = jnp.cos(angle)
    table_ref[1] = jnp.where(lane < HALF_DIM, -1.0, 1.0) * jnp.sin(angle)
    copies[0].wait()
    for m in range(groups):
        for side in range(2):
            block = (parity ^ side) * groups + (group ^ m)
            outs[m][side] = put(own_hot, v_buffer[:, lanes(block, wide)])
    for t in range(2):
        copies[1 + t].wait()
        for h in range(heads):
            out_ref[t, :, lanes(h)] = put(own_hot, rotated(kq_buffer[t, :, lanes(h)], table_ref, 1))


def gate_kernel(counts, weight_ref, input_ref, g_ref, out_ref, gate_ref):
    cap, half = out_ref.shape
    parity = own_place(counts)[0]
    own_hot, _ = places(counts, cap)
    total = jnp.zeros((cap, HEAD_DIM), F32)
    for b in range(input_ref.shape[1] // HEAD_DIM):
        total += input_ref[:, lanes(b)].astype(F32) * weight_ref[0:1, lanes(b)].astype(F32)
    logit = jnp.sum(total, axis=1, keepdims=True)
    gate = jnp.broadcast_to(1.0 / (1.0 + jnp.exp(-logit)), (cap, HEAD_DIM))
    gate_ref[...] = gate
    heads = half // HEAD_DIM
    for h in range(heads):
        rows = g_ref[:, lanes((1 - parity) * heads + h)].astype(F32) * gate
        out_ref[:, lanes(h)] = put(own_hot, rows.astype(BF16))


def pack_kernel(groups, counts, table_ref, k_ref, q_ref, in_ref, *outs):
    cap, half = in_ref.shape[1:]
    parity, group, _ = own_place(counts)
    own_hot, _ = places(counts, cap)
    heads = half // groups // HEAD_DIM
    for m in range(groups):
        for t, ref in enumerate((k_ref, q_ref)):
            for c in range(heads):
                h = (group ^ m) * heads + c
                rows = rotated(ref[:, lanes(parity * groups * heads + h)], table_ref, 1)
                outs[m][t, :, lanes(c)] = put(own_hot, rows) + in_ref[t, :, lanes(h)]


def pack_gated_kernel(groups, counts, gate_ref, g_ref, in_ref, v_own_ref, v_in_ref, *refs):
    outs, v_ref = refs[:groups], refs[groups]
    cap, half = in_ref.shape
    parity, group, _ = own_place(counts)
    own_hot, _ = places(counts, cap)
    heads = half // groups // HEAD_DIM
    for m in range(groups):
        for c in range(heads):
            h = (group ^ m) * heads + c
            rows = g_ref[:, lanes(parity * groups * heads + h)].astype(F32) * gate_ref[...]
            outs[m][:, lanes(c)] = put(own_hot, rows.astype(BF16)) + in_ref[:, lanes(h)]
    v_ref[...] = v_own_ref[...] + v_in_ref[...]


def block_of(m, cap):
    return pl.ds(pl.multiple_of(((lax.axis_index("seq") >> 1) ^ m) * cap, cap), cap)


def gather_values_kernel(groups, counts, *refs):
    own_ref, send_ref = refs[groups:]
    cap = refs[0].shape[1]
    for i in range(groups):
        block = block_of(groups - 1 - i, cap)
        own_ref[block, :] = refs[i][0]
        send_ref[block, :] = refs[i][1]


def gather_kernel(groups, counts, *refs):
    cap = refs[0].shape[1]
    for i in range(groups):
        refs[groups][:, block_of(groups - 1 - i, cap), :] = refs[i][...]


def probabilities_kernel(groups, counts, kq_ref, v_ref, *refs):
    g_refs, (ds_ref, dv_ref, delta_ref, g_ref, sum_ref) = refs[:groups], refs[groups:]
    cap, wide = g_refs[0].shape
    for i in range(groups):
        g_ref[block_of(groups - 1 - i, cap), :] = g_refs[i][...]
    key, query = grid_of(cap)
    kept = query >= key
    for c in range(wide // HEAD_DIM):
        sum_ref[...] = jnp.zeros_like(sum_ref)
        for i in range(groups):
            upto = (i + 1) * cap
            here = slice(i * cap, upto)
            g = g_ref[here, lanes(c)]
            s = dot(kq_ref[0, :upto, lanes(c)], kq_ref[1, here, lanes(c)], ((1,), (1,))) * SCALE
            last = jnp.where(kept, s[i * cap:], NEG)
            s = last if i == 0 else jnp.concatenate([s[:i * cap], last], axis=0)
            e = jnp.exp(s - jnp.max(s, axis=0, keepdims=True))
            p = e * (1.0 / jnp.sum(e, axis=0, keepdims=True))
            dp = dot(v_ref[:upto, lanes(c)], g, ((1,), (1,)))
            delta = jnp.sum(p * dp, axis=0, keepdims=True)
            whole = jnp.broadcast_to(delta, (8, cap))
            delta_ref[i] = whole if c == 0 else delta_ref[i] + whole
            p16 = p.astype(BF16)
            ds_ref[c, i, :upto, :] = (p16.astype(F32) * (dp - delta) * SCALE).astype(BF16)
            sum_ref[:upto, :] += dot(p16, g, ((1,), (0,)))
        dv_ref[:, lanes(c)] = sum_ref[...].astype(BF16)


def gradients_kernel(groups, counts, kq_ref, ds_ref, delta_ref, *refs):
    outs, (dq_ref, dk_ref) = refs[:groups], refs[groups:]
    heads, _, total, cap = ds_ref.shape
    for c in range(heads):
        dk_ref[...] = jnp.zeros_like(dk_ref)
        for i in range(groups):
            upto = (i + 1) * cap
            here = slice(i * cap, upto)
            ds = ds_ref[c, i, :upto, :]
            dk_ref[:upto, :] += dot(ds, kq_ref[1, here, lanes(c)], ((1,), (0,)))
            dq_ref[here, :] = dot(ds, kq_ref[0, :upto, lanes(c)], ((0,), (0,)))
        for m in range(groups):
            block = block_of(m, cap)
            outs[m][0:cap, lanes(c)] = dq_ref[block, :].astype(BF16)
            outs[m][cap:2 * cap, lanes(c)] = dk_ref[block, :].astype(BF16)
    line = lax.broadcasted_iota(jnp.int32, (8, cap), 0)
    for m in range(groups):
        delta = delta_ref[own_place(counts)[1] ^ m]
        coarse = delta.astype(BF16).astype(F32)
        rows = jnp.where(line == 0, coarse, jnp.where(line == 1, delta - coarse, 0.0))
        rows = jnp.concatenate([rows, jnp.zeros_like(rows)], axis=0).astype(BF16)
        for c in range(heads):
            outs[m][2 * cap:, lanes(c)] = rows


def delta_kernel(groups, *refs):
    ins, out_ref = refs[:groups], refs[groups]
    rows = ins[0].shape[0]
    total = ins[0][rows - 16:, 0:HEAD_DIM].astype(F32)
    for ref in ins[1:]:
        total += ref[rows - 16:, 0:HEAD_DIM].astype(F32)
    out_ref[...] = jnp.broadcast_to(total[0:1, :] + total[1:2, :], out_ref.shape)


def unpack_kernel(groups, counts, table_ref, dv_ref, dv_in_ref, *refs):
    ins, own_ref, send_ref, outs = refs[:groups], refs[groups], refs[groups + 1], refs[groups + 2:]
    cap = own_ref.shape[1]
    for m in range(groups):
        block = block_of(m, cap)
        outs[m][0] = dv_ref[block, :]
        outs[m][1] = dv_in_ref[block, :]
    wide = ins[0].shape[1]
    heads = wide // HEAD_DIM
    own_hot, in_hot = places(counts, cap)
    for i in range(groups):
        group = own_place(counts)[1] ^ (groups - 1 - i)
        for t in range(2):
            send_ref[t, :, lanes(group, wide)] = taken(in_hot, ins[i][t * cap:(t + 1) * cap, :])
            for c in range(heads):
                own = dot(own_hot, ins[i][t * cap:(t + 1) * cap, lanes(c)], ((0,), (0,)))
                own_ref[t, :, lanes(group * heads + c)] = rotated(own, table_ref, -1)


def router_kernel(counts, delta_ref, delta_in_ref, gate_ref, input_ref, out_ref):
    cap = input_ref.shape[0]
    parity, _, count = own_place(counts)
    row, column = grid_of(cap)
    start = jnp.where(parity == 0, 0, cap - count)
    delta = delta_ref[0:1, :] + delta_in_ref[0:1, :]
    own = jnp.where((column == row + start) & (row < count), delta, 0.0)
    term = (1.0 - gate_ref[...]) * jnp.sum(own, axis=1, keepdims=True)
    for b in range(out_ref.shape[0]):
        out_ref[b:b + 1, :] = jnp.sum(input_ref[:, lanes(b)].astype(F32) * term, axis=0, keepdims=True)


def place_kernel(groups, counts, table_ref, own_ref, in_ref, *refs):
    ins, outs, (buffer, sems) = refs[:groups], refs[groups:groups + 3], refs[groups + 3:]
    cap, wide = ins[0].shape[1:]
    half = own_ref.shape[2]
    heads = half // HEAD_DIM
    parity, group, _ = own_place(counts)
    own_hot, _ = places(counts, cap)
    copies = [
        pltpu.make_async_copy(own_ref.at[t], outs[t].at[:, lanes(parity, half)], sems.at[t]) for t in range(2)
    ]
    for copy in copies:
        copy.start()
    for t in range(2):
        for h in range(heads):
            buffer[t, :, lanes(h)] = rotated(in_ref[t, :, lanes(h)], table_ref, -1)
        copies.append(pltpu.make_async_copy(buffer.at[t], outs[t].at[:, lanes(1 - parity, half)], sems.at[2 + t]))
        copies[-1].start()
    for side in range(2):
        for i in range(groups):
            buffer[2 + side, :, lanes(group ^ (groups - 1 - i), wide)] = taken(own_hot, ins[i][side])
        copies.append(pltpu.make_async_copy(buffer.at[2 + side], outs[2].at[:, lanes(parity ^ side, half)], sems.at[4 + side]))
        copies[-1].start()
    for copy in copies:
        copy.wait()


def per_device(queries, key_rows, value_rows, out_grad, inputs, router_weight, counts, picked_pos):
    query_own, key_own, value_own, grad_own, input_own = queries[0], key_rows[0], value_rows[0], out_grad[0], inputs[0]
    cap, width = query_own.shape
    half = width // 2
    seq_size = lax.axis_size("seq")
    groups = seq_size // 2
    wide = half // groups
    total = groups * cap
    heads = wide // HEAD_DIM

    def kernel(body):
        return functools.partial(body, groups)

    *values, sent, table = pl.pallas_call(
        kernel(front_kernel),
        in_specs=[SMEM, VMEM] + [ANY] * 3,
        out_specs=[VMEM] * (groups + 2),
        out_shape=[jax.ShapeDtypeStruct((2, cap, wide), BF16)] * groups
        + [jax.ShapeDtypeStruct((2, cap, half), BF16), jax.ShapeDtypeStruct((2, cap, HEAD_DIM), F32)],
        scratch_shapes=[
            pltpu.VMEM((cap, width), BF16), pltpu.VMEM((2, cap, half), BF16), pltpu.SemaphoreType.DMA((3,)),
        ],
        compiler_params=pltpu.CompilerParams(vmem_limit_bytes=FRONT * 1024 * 1024),
        cost_estimate=SMALL,
        name="front",
    )(counts, picked_pos, value_own, key_own, query_own)
    kq_in = swapped(sent)
    values = spread(values)
    router_full = lax.all_gather(after(router_weight, table), "fsdp", axis=0, tiled=True)
    sent, gate = call(
        gate_kernel, "gate", [((cap, half), BF16), ((cap, HEAD_DIM), F32)], counts, router_full[None, :], input_own, grad_own
    )
    g_in = swapped(sent)
    v_own, sent = call(kernel(gather_values_kernel), "gather_values", [((total, wide), BF16)] * 2, counts, *values)
    v_in = swapped(sent)
    kq = spread(call(
        kernel(pack_kernel),
        "pack",
        [((2, cap, wide), BF16)] * groups,
        after(counts, v_own), table, key_own, query_own, kq_in,
    ))
    *gated, v = call(
        kernel(pack_gated_kernel),
        "pack_gated",
        [((cap, wide), BF16)] * groups + [((total, wide), BF16)],
        after(counts, kq[-1]), gate, grad_own, g_in, v_own, v_in,
    )
    gated = spread(gated)
    (kq,) = call(kernel(gather_kernel), "gather", [((2, total, wide), BF16)], counts, *kq, cost_estimate=LARGE)

    ds, dv, delta = call(
        kernel(probabilities_kernel),
        "probabilities",
        [((heads, groups, total, cap), BF16), ((total, wide), BF16), ((groups, 8, cap), F32)],
        counts, kq, v, *gated,
        scratch_shapes=[pltpu.VMEM((total, wide), BF16), pltpu.VMEM((total, HEAD_DIM), F32)],
    )
    dv_in = swapped(dv)
    pieces = spread(call(
        kernel(gradients_kernel),
        "gradients",
        [((2 * cap + 16, wide), BF16)] * groups,
        counts, kq, ds, delta,
        scratch_shapes=[pltpu.VMEM((total, HEAD_DIM), F32)] * 2,
    ))
    (delta,) = call(kernel(delta_kernel), "delta", [((8, cap), F32)], *pieces)
    delta_in = swapped(delta)
    own, sent, *v_pieces = call(
        kernel(unpack_kernel),
        "unpack",
        [((2, cap, half), BF16)] * 2 + [((2, cap, wide), BF16)] * groups,
        after(counts, delta), table, dv, dv_in, *pieces,
    )
    other = swapped(sent)
    (part,) = call(
        router_kernel, "router", [((input_own.shape[1] // HEAD_DIM, HEAD_DIM), F32)],
        after(counts, own), delta, delta_in, gate, input_own,
    )
    devices = seq_size * lax.axis_size("fsdp")
    shares = lax.all_to_all(part.reshape(devices, -1), ("seq", "fsdp"), 0, 0)
    grad_router = jnp.sum(shares, axis=0)
    v_pieces = spread(v_pieces)
    grad_q, grad_k, grad_v = pl.pallas_call(
        kernel(place_kernel),
        in_specs=[SMEM] + [VMEM] * (3 + groups),
        out_specs=[ANY] * 3,
        out_shape=[jax.ShapeDtypeStruct((cap, width), BF16)] * 3,
        scratch_shapes=[pltpu.VMEM((4, cap, half), BF16), pltpu.SemaphoreType.DMA((6,))],
        compiler_params=PARAMS,
        cost_estimate=SMALL,
        name="place",
    )(counts, table, own, other, *v_pieces)
    return grad_q[None], grad_k[None], grad_v[None], grad_router


def solution(mesh):
    rows = P("fsdp", "seq", None)
    placed = (rows, rows, rows, rows, rows, P("fsdp"), P("fsdp", "seq"), P("fsdp", "seq"))
    return jax.shard_map(
        per_device,
        mesh=mesh,
        in_specs=placed,
        out_specs=(rows, rows, rows, P(("seq", "fsdp"))),
        check_vma=False,
    )
```

```python
import functools
import math

import jax
import jax.numpy as jnp
from jax import lax
from jax.experimental import pallas as pl
from jax.experimental.pallas import tpu as pltpu
from jax.sharding import PartitionSpec as P

HEADS = 16
HEAD_DIM = 128
HALF_DIM = HEAD_DIM // 2
TOK_DEV = 512
THETA = 500000.0
NEG = -1e30
SCALE = HEAD_DIM ** -0.5
BF16 = jnp.bfloat16
F32 = jnp.float32
PARAMS = pltpu.CompilerParams(vmem_limit_bytes=40 * 1024 * 1024)
FRONT = 63
COSTS = {"gather": 0.3, "unpack_values": 1, "gate": 1}
VMEM = pl.BlockSpec(memory_space=pltpu.VMEM)
ANY = pl.BlockSpec(memory_space=pl.ANY)
SMEM = pl.BlockSpec(memory_space=pltpu.SMEM)


def swapped(array):
    return lax.ppermute(array, "seq", [(i, i ^ 1) for i in range(lax.axis_size("seq"))])


def spread(pieces):
    size = lax.axis_size("seq")
    arrived = [
        lax.ppermute(pieces[m], "seq", [(i, i ^ (2 * m)) for i in range(size)]) for m in range(len(pieces) - 1, 0, -1)
    ]
    return arrived + [pieces[0]]


def cost(name):
    return pl.CostEstimate(flops=int(COSTS.get(name, 0.001) * 1e9), bytes_accessed=1 << 16, transcendentals=0)


def call(kernel, name, shapes, *operands, wait=(), scratch_shapes=()):
    count = len(operands)

    def body(*refs):
        kernel(*refs[:count], *refs[count + len(wait):])

    return pl.pallas_call(
        body,
        in_specs=[SMEM if a.shape == (1, 1) else VMEM for a in operands] + [ANY] * len(wait),
        out_specs=[VMEM] * len(shapes),
        out_shape=[jax.ShapeDtypeStruct(shape, dtype) for shape, dtype in shapes],
        scratch_shapes=scratch_shapes,
        compiler_params=PARAMS,
        cost_estimate=cost(name),
        name=name,
    )(*operands, *wait)


def dot(a, b, contract):
    return lax.dot_general(a, b, ((contract[0], contract[1]), ((), ())), preferred_element_type=F32)


def lanes(index, width=HEAD_DIM):
    if isinstance(index, int):
        return slice(index * width, (index + 1) * width)
    return pl.ds(pl.multiple_of(index * width, HEAD_DIM), width)


def grid_of(cap):
    row = lax.broadcasted_iota(jnp.int32, (cap, cap), 0)
    column = lax.broadcasted_iota(jnp.int32, (cap, cap), 1)
    return row, column


def own_place(counts):
    index = lax.axis_index("seq")
    return index & 1, index >> 1, counts[0, 0]


def places(counts, cap):
    parity, _, count = own_place(counts)
    first = jnp.where(parity == 0, count, cap - count)
    row, slot = grid_of(cap)
    even = jnp.where((row == slot) & (row < first), 1.0, 0.0)
    odd = jnp.where((row == slot + first) & (row >= first), 1.0, 0.0)
    is_even = parity == 0
    return jnp.where(is_even, even, odd).astype(BF16), jnp.where(is_even, odd, even).astype(BF16)


def rotated(rows, table_ref, direction):
    rows = rows.astype(F32)
    turned = pltpu.roll(rows, HALF_DIM, 1) * table_ref[1]
    rows = rows * table_ref[0]
    return (rows + turned if direction > 0 else rows - turned).astype(BF16)


def put(hot, rows):
    return dot(hot, rows, ((1,), (0,))).astype(BF16)


def taken(hot, rows):
    return dot(hot, rows, ((0,), (0,))).astype(BF16)


def front_kernel(groups, counts, pos_ref, v_ref, k_ref, q_ref, *refs):
    outs, (out_ref, table_ref, v_buffer, kq_buffer, sems) = refs[:groups], refs[groups:]
    cap, half = out_ref.shape[1:]
    wide = outs[0].shape[2]
    heads = half // HEAD_DIM
    parity, group, _ = own_place(counts)
    copies = [pltpu.make_async_copy(v_ref, v_buffer, sems.at[0])]
    for t, ref in enumerate((k_ref, q_ref)):
        copies.append(pltpu.make_async_copy(ref.at[:, lanes(1 - parity, half)], kq_buffer.at[t], sems.at[1 + t]))
    for copy in copies:
        copy.start()
    own_hot, _ = places(counts, cap)
    row, column = grid_of(cap)
    position = (lax.axis_index("seq") * TOK_DEV + pos_ref[0:1, :]).astype(F32)
    position = jnp.sum(jnp.where(row == column, position, 0.0), axis=1, keepdims=True)
    lane = lax.broadcasted_iota(jnp.int32, (cap, HEAD_DIM), 1)
    feature = jnp.where(lane < HALF_DIM, lane, lane - HALF_DIM).astype(F32)
    angle = position * jnp.exp(feature * (-2.0 / HEAD_DIM * math.log(THETA)))
    table_ref[0] = jnp.cos(angle)
    table_ref[1] = jnp.where(lane < HALF_DIM, -1.0, 1.0) * jnp.sin(angle)
    copies[0].wait()
    for m in range(groups):
        for side in range(2):
            block = (parity ^ side) * groups + (group ^ m)
            outs[m][side] = put(own_hot, v_buffer[:, lanes(block, wide)])
    for t in range(2):
        copies[1 + t].wait()
        for h in range(heads):
            out_ref[t, :, lanes(h)] = put(own_hot, rotated(kq_buffer[t, :, lanes(h)], table_ref, 1))


def gate_kernel(counts, weight_ref, input_ref, g_ref, out_ref, gate_ref):
    cap, half = out_ref.shape
    parity = own_place(counts)[0]
    own_hot, _ = places(counts, cap)
    total = jnp.zeros((cap, HEAD_DIM), F32)
    for b in range(input_ref.shape[1] // HEAD_DIM):
        total += input_ref[:, lanes(b)].astype(F32) * weight_ref[0:1, lanes(b)].astype(F32)
    logit = jnp.sum(total, axis=1, keepdims=True)
    gate = jnp.broadcast_to(1.0 / (1.0 + jnp.exp(-logit)), (cap, HEAD_DIM))
    gate_ref[...] = gate
    heads = half // HEAD_DIM
    for h in range(heads):
        rows = g_ref[:, lanes((1 - parity) * heads + h)].astype(F32) * gate
        out_ref[:, lanes(h)] = put(own_hot, rows.astype(BF16))


def pack_kernel(groups, counts, table_ref, k_ref, q_ref, in_ref, *outs):
    cap, half = in_ref.shape[1:]
    parity, group, _ = own_place(counts)
    own_hot, _ = places(counts, cap)
    heads = half // groups // HEAD_DIM
    for m in range(groups):
        for t, ref in enumerate((k_ref, q_ref)):
            for c in range(heads):
                h = (group ^ m) * heads + c
                rows = rotated(ref[:, lanes(parity * groups * heads + h)], table_ref, 1)
                outs[m][t, :, lanes(c)] = put(own_hot, rows) + in_ref[t, :, lanes(h)]


def pack_gated_kernel(groups, counts, gate_ref, g_ref, in_ref, *outs):
    cap, half = in_ref.shape
    parity, group, _ = own_place(counts)
    own_hot, _ = places(counts, cap)
    heads = half // groups // HEAD_DIM
    for m in range(groups):
        for c in range(heads):
            h = (group ^ m) * heads + c
            rows = g_ref[:, lanes(parity * groups * heads + h)].astype(F32) * gate_ref[...]
            outs[m][:, lanes(c)] = put(own_hot, rows.astype(BF16)) + in_ref[:, lanes(h)]


def block_of(m, cap):
    return pl.ds(pl.multiple_of(((lax.axis_index("seq") >> 1) ^ m) * cap, cap), cap)


def gather_values_kernel(groups, counts, *refs):
    own_ref, send_ref = refs[groups:]
    cap = refs[0].shape[1]
    for i in range(groups):
        block = block_of(groups - 1 - i, cap)
        own_ref[block, :] = refs[i][0]
        send_ref[block, :] = refs[i][1]


def gather_kernel(groups, counts, v_own_ref, v_in_ref, *refs):
    cap = refs[0].shape[1]
    for i in range(groups):
        refs[groups][0:2, block_of(groups - 1 - i, cap), :] = refs[i][...]
    refs[groups][2] = v_own_ref[...] + v_in_ref[...]


def probabilities_kernel(groups, counts, kqv_ref, *refs):
    g_refs, outs, (ds_ref, delta_ref, g_ref, sum_ref) = refs[:groups], refs[groups:2 * groups], refs[2 * groups:]
    cap, wide = g_refs[0].shape
    for i in range(groups):
        g_ref[block_of(groups - 1 - i, cap), :] = g_refs[i][...]
    key, query = grid_of(cap)
    kept = query >= key
    for c in range(wide // HEAD_DIM):
        sum_ref[...] = jnp.zeros_like(sum_ref)
        for i in range(groups):
            upto = (i + 1) * cap
            here = slice(i * cap, upto)
            g = g_ref[here, lanes(c)]
            s = dot(kqv_ref[0, :upto, lanes(c)], kqv_ref[1, here, lanes(c)], ((1,), (1,))) * SCALE
            last = jnp.where(kept, s[i * cap:], NEG)
            s = last if i == 0 else jnp.concatenate([s[:i * cap], last], axis=0)
            e = jnp.exp(s - jnp.max(s, axis=0, keepdims=True))
            p = e * (1.0 / jnp.sum(e, axis=0, keepdims=True))
            dp = dot(kqv_ref[2, :upto, lanes(c)], g, ((1,), (1,)))
            delta = jnp.sum(p * dp, axis=0, keepdims=True)
            whole = jnp.broadcast_to(delta, (8, cap))
            delta_ref[i] = whole if c == 0 else delta_ref[i] + whole
            p16 = p.astype(BF16)
            ds_ref[c, i, :upto, :] = (p16.astype(F32) * (dp - delta) * SCALE).astype(BF16)
            sum_ref[:upto, :] += dot(p16, g, ((1,), (0,)))
        for m in range(groups):
            outs[m][:, lanes(c)] = sum_ref[block_of(m, cap), :].astype(BF16)


def grad_keys_kernel(groups, counts, kqv_ref, ds_ref, *refs):
    deltas, outs, sum_ref = refs[:-groups - 1], refs[-groups - 1:-1], refs[-1]
    heads, _, total, cap = ds_ref.shape
    for c in range(heads):
        sum_ref[...] = jnp.zeros_like(sum_ref)
        for i in range(groups):
            upto = (i + 1) * cap
            sum_ref[:upto, :] += dot(ds_ref[c, i, :upto, :], kqv_ref[1, i * cap:upto, lanes(c)], ((1,), (0,)))
        for m in range(groups):
            outs[m][0:cap, lanes(c)] = sum_ref[block_of(m, cap), :].astype(BF16)
    line = lax.broadcasted_iota(jnp.int32, (8, cap), 0)
    for m in range(groups):
        group = own_place(counts)[1] ^ m
        delta = sum(ref[group] for ref in deltas)
        coarse = delta.astype(BF16).astype(F32)
        rows = jnp.where(line == 0, coarse, jnp.where(line == 1, delta - coarse, 0.0))
        rows = jnp.concatenate([rows, jnp.zeros_like(rows)], axis=0).astype(BF16)
        for c in range(heads):
            outs[m][cap:, lanes(c)] = rows


def grad_queries_kernel(groups, counts, kqv_ref, ds_ref, *refs):
    outs, sum_ref = refs[:groups], refs[groups]
    heads, _, total, cap = ds_ref.shape
    for c in range(heads):
        for i in range(groups):
            upto = (i + 1) * cap
            sum_ref[i * cap:upto, :] = dot(ds_ref[c, i, :upto, :], kqv_ref[0, :upto, lanes(c)], ((0,), (0,)))
        for m in range(groups):
            outs[m][:, lanes(c)] = sum_ref[block_of(m, cap), :].astype(BF16)


def unpack_kernel(groups, turned, counts, table_ref, *refs):
    ins, own_ref, send_ref, token_ref = refs[:groups], refs[groups], refs[groups + 1], refs[groups + 2]
    cap = own_ref.shape[0]
    wide = ins[0].shape[1]
    heads = wide // HEAD_DIM
    own_hot, in_hot = places(counts, cap)
    for i in range(groups):
        group = own_place(counts)[1] ^ (groups - 1 - i)
        send_ref[:, lanes(group, wide)] = taken(in_hot, ins[i][0:cap, :])
        for c in range(heads):
            own = dot(own_hot, ins[i][0:cap, lanes(c)], ((0,), (0,)))
            own_ref[:, lanes(group * heads + c)] = rotated(own, table_ref, -1) if turned else own.astype(BF16)
    token_ref[...] = jnp.zeros_like(token_ref)


def delta_kernel(*refs):
    ins, out_ref = refs[:-1], refs[-1]
    rows = ins[0].shape[0]
    total = ins[0][rows - 16:, 0:HEAD_DIM].astype(F32)
    for ref in ins[1:]:
        total += ref[rows - 16:, 0:HEAD_DIM].astype(F32)
    out_ref[...] = jnp.broadcast_to(total[0:1, :] + total[1:2, :], out_ref.shape)


def router_kernel(counts, gate_ref, input_ref, *refs):
    deltas, out_ref = refs[:-1], refs[-1]
    cap = input_ref.shape[0]
    parity, _, count = own_place(counts)
    row, column = grid_of(cap)
    start = jnp.where(parity == 0, 0, cap - count)
    own = jnp.where((column == row + start) & (row < count), sum(ref[0:1, :] for ref in deltas), 0.0)
    term = (1.0 - gate_ref[...]) * jnp.sum(own, axis=1, keepdims=True)
    for b in range(out_ref.shape[0]):
        out_ref[b:b + 1, :] = jnp.sum(input_ref[:, lanes(b)].astype(F32) * term, axis=0, keepdims=True)


def total_kernel(in_ref, out_ref):
    out_ref[...] = jnp.sum(in_ref[...], axis=0, keepdims=True)


def place_kernel(turned, counts, table_ref, own_ref, in_ref, out_ref, token_ref):
    half = own_ref.shape[1]
    heads = half // HEAD_DIM
    parity = own_place(counts)[0]
    out_ref[:, lanes(parity, half)] = own_ref[...]
    token_ref[...] = jnp.zeros_like(token_ref)
    if not turned:
        out_ref[:, lanes(1 - parity, half)] = in_ref[...]
        return
    for h in range(heads):
        out_ref[:, lanes((1 - parity) * heads + h)] = rotated(in_ref[:, lanes(h)], table_ref, -1)


def per_device(queries, key_rows, value_rows, out_grad, inputs, router_weight, counts, picked_pos):
    query_own, key_own, value_own, grad_own, input_own = queries[0], key_rows[0], value_rows[0], out_grad[0], inputs[0]
    cap, width = query_own.shape
    half = width // 2
    seq_size = lax.axis_size("seq")
    groups = seq_size // 2
    wide = half // groups
    total = groups * cap
    heads = wide // HEAD_DIM

    def kernel(body):
        return functools.partial(body, groups)

    *values, sent, table = pl.pallas_call(
        kernel(front_kernel),
        in_specs=[SMEM, VMEM] + [ANY] * 3,
        out_specs=[VMEM] * (groups + 2),
        out_shape=[jax.ShapeDtypeStruct((2, cap, wide), BF16)] * groups
        + [jax.ShapeDtypeStruct((2, cap, half), BF16), jax.ShapeDtypeStruct((2, cap, HEAD_DIM), F32)],
        scratch_shapes=[
            pltpu.VMEM((cap, width), BF16), pltpu.VMEM((2, cap, half), BF16), pltpu.SemaphoreType.DMA((3,)),
        ],
        compiler_params=pltpu.CompilerParams(vmem_limit_bytes=FRONT * 1024 * 1024),
        cost_estimate=cost("front"),
        name="front",
    )(counts, picked_pos, value_own, key_own, query_own)
    kq_in = swapped(sent)
    values = spread(values)
    router_full = lax.all_gather(router_weight, "fsdp", axis=0, tiled=True)
    sent, gate = call(
        gate_kernel, "gate", [((cap, half), BF16), ((cap, HEAD_DIM), F32)], counts, router_full[None, :], input_own, grad_own
    )
    g_in = swapped(sent)
    kq = spread(call(
        kernel(pack_kernel),
        "pack",
        [((2, cap, wide), BF16)] * groups,
        counts, table, key_own, query_own, kq_in,
    ))
    v_own, sent = call(
        kernel(gather_values_kernel), "gather_values", [((total, wide), BF16)] * 2, counts, *values, wait=kq[-1:]
    )
    v_in = swapped(sent)
    gated = spread(call(
        kernel(pack_gated_kernel),
        "pack_gated",
        [((cap, wide), BF16)] * groups,
        counts, gate, grad_own, g_in, wait=[v_own],
    ))
    kqv = call(
        kernel(gather_kernel), "gather", [((3, total, wide), BF16)], counts, v_own, v_in, *kq
    )[0]

    piece = ((cap, wide), BF16)
    *pieces, ds, delta = call(
        kernel(probabilities_kernel),
        "probabilities",
        [piece] * groups + [((heads, groups, total, cap), BF16), ((groups, 8, cap), F32)],
        counts, kqv, *gated,
        scratch_shapes=[pltpu.VMEM((total, wide), BF16), pltpu.VMEM((total, HEAD_DIM), F32)],
    )
    v_pieces = spread(pieces)
    k_pieces = spread(call(
        kernel(grad_keys_kernel),
        "grad_keys",
        [((cap + 16, wide), BF16)] * groups,
        counts, kqv, ds, delta,
        scratch_shapes=[pltpu.VMEM((total, HEAD_DIM), F32)],
    ))

    def unpacked(name, turned, pieces, wait=()):
        shapes = [((cap, half), BF16)] * 2 + [((8, cap), F32)]
        return call(functools.partial(unpack_kernel, groups, turned), name, shapes, counts, table, *pieces, wait=wait)

    def placed(name, turned, own, other, wait):
        body = functools.partial(place_kernel, turned)
        return call(body, name, [((cap, width), BF16), ((8, HEAD_DIM), F32)], counts, table, own, other, wait=wait)

    v_own, sent, token = unpacked("unpack_values", False, v_pieces, k_pieces[-1:])
    v_in = swapped(sent)
    grad_v, token_v = placed("place_values", False, v_own, v_in, [])
    q_pieces = spread(call(
        kernel(grad_queries_kernel),
        "grad_queries",
        [piece] * groups,
        counts, kqv, ds,
        wait=[token],
        scratch_shapes=[pltpu.VMEM((total, HEAD_DIM), F32)],
    ))
    (delta,) = call(delta_kernel, "delta", [((8, cap), F32)], *k_pieces)
    delta_in = swapped(delta)
    k_own, sent, token_k = unpacked("unpack_keys", True, k_pieces, q_pieces[:1])
    k_in = swapped(sent)
    (part,) = call(
        router_kernel, "router", [((input_own.shape[1] // HEAD_DIM, HEAD_DIM), F32)], counts, gate, input_own, delta, delta_in,
        wait=[token_k],
    )
    q_own, sent, _ = unpacked("unpack_queries", True, q_pieces, [part])
    q_in = swapped(sent)
    grad_k, token_k = placed("place_keys", True, k_own, k_in, [token_v])
    grad_q, _ = placed("place_queries", True, q_own, q_in, [token_k])
    devices = seq_size * lax.axis_size("fsdp")
    shares = lax.all_to_all(part.reshape(devices, -1), ("seq", "fsdp"), 0, 0, tiled=True)
    grad_router = call(total_kernel, "total", [((1, shares.shape[1]), F32)], shares, wait=[token_k])[0][0]
    return grad_q[None], grad_k[None], grad_v[None], grad_router


def solution(mesh):
    rows = P("fsdp", "seq", None)
    placed = (rows, rows, rows, rows, rows, P("fsdp"), P("fsdp", "seq"), P("fsdp", "seq"))
    return jax.shard_map(
        per_device,
        mesh=mesh,
        in_specs=placed,
        out_specs=(rows, rows, rows, P(("seq", "fsdp"))),
        check_vma=False,
    )
```

```python
import functools
import math

import jax
import jax.numpy as jnp
from jax import lax
from jax.experimental import pallas as pl
from jax.experimental.pallas import tpu as pltpu
from jax.sharding import PartitionSpec as P

HEADS = 16
HEAD_DIM = 128
HALF_DIM = HEAD_DIM // 2
TOK_DEV = 512
THETA = 500000.0
NEG = -1e30
SCALE = HEAD_DIM ** -0.5
BF16 = jnp.bfloat16
F32 = jnp.float32
PARAMS = pltpu.CompilerParams(vmem_limit_bytes=40 * 1024 * 1024)
COSTS = {"gather": 0.3, "gate": 1, "place_keys": 0.5, "router": 1}
VMEM = pl.BlockSpec(memory_space=pltpu.VMEM)
ANY = pl.BlockSpec(memory_space=pl.ANY)
HBM = pl.BlockSpec(memory_space=pltpu.HBM)
SMEM = pl.BlockSpec(memory_space=pltpu.SMEM)


def swapped(array):
    return lax.ppermute(array, "seq", [(i, i ^ 1) for i in range(lax.axis_size("seq"))])


def spread(pieces):
    size = lax.axis_size("seq")
    arrived = [
        lax.ppermute(pieces[m], "seq", [(i, i ^ (2 * m)) for i in range(size)]) for m in range(len(pieces) - 1, 0, -1)
    ]
    return arrived + [pieces[0]]


def cost(name):
    return pl.CostEstimate(flops=int(COSTS.get(name, 0.001) * 1e9), bytes_accessed=1 << 16, transcendentals=0)


def call(kernel, name, shapes, *operands, wait=(), scratch_shapes=()):
    count = len(operands)

    def body(*refs):
        kernel(*refs[:count], *refs[count + len(wait):])

    return pl.pallas_call(
        body,
        in_specs=[SMEM if a.shape == (1, 1) else VMEM for a in operands] + [ANY] * len(wait),
        out_specs=[VMEM] * len(shapes),
        out_shape=[jax.ShapeDtypeStruct(shape, dtype) for shape, dtype in shapes],
        scratch_shapes=scratch_shapes,
        compiler_params=PARAMS,
        cost_estimate=cost(name),
        name=name,
    )(*operands, *wait)


def dot(a, b, contract):
    return lax.dot_general(a, b, ((contract[0], contract[1]), ((), ())), preferred_element_type=F32)


def lanes(index, width=HEAD_DIM):
    if isinstance(index, int):
        return slice(index * width, (index + 1) * width)
    return pl.ds(pl.multiple_of(index * width, HEAD_DIM), width)


def grid_of(cap):
    row = lax.broadcasted_iota(jnp.int32, (cap, cap), 0)
    column = lax.broadcasted_iota(jnp.int32, (cap, cap), 1)
    return row, column


def own_place(counts):
    index = lax.axis_index("seq")
    return index & 1, index >> 1, counts[0, 0]


def places(counts, cap):
    parity, _, count = own_place(counts)
    first = jnp.where(parity == 0, count, cap - count)
    row, slot = grid_of(cap)
    even = jnp.where((row == slot) & (row < first), 1.0, 0.0)
    odd = jnp.where((row == slot + first) & (row >= first), 1.0, 0.0)
    is_even = parity == 0
    return jnp.where(is_even, even, odd).astype(BF16), jnp.where(is_even, odd, even).astype(BF16)


def rotated(rows, table_ref, direction):
    rows = rows.astype(F32)
    turned = pltpu.roll(rows, HALF_DIM, 1) * table_ref[1]
    rows = rows * table_ref[0]
    return (rows + turned if direction > 0 else rows - turned).astype(BF16)


def put(hot, rows):
    return dot(hot, rows, ((1,), (0,))).astype(BF16)


def taken(hot, rows):
    return dot(hot, rows, ((0,), (0,))).astype(BF16)


def front_kernel(groups, counts, pos_ref, v_ref, k_ref, q_ref, *refs):
    outs, out_ref, table_ref = refs[:groups], refs[groups], refs[groups + 1]
    pos, v_buffer, kq_buffer, sems = refs[groups + 2:]
    cap, half = out_ref.shape[1:]
    wide = outs[0].shape[2]
    heads = half // HEAD_DIM
    index = lax.axis_index("seq")
    parity, group = index & 1, index >> 1
    small = [pltpu.make_async_copy(pos_ref, pos, sems.at[1])]
    large = [
        pltpu.make_async_copy(ref.at[:, lanes(1 - parity, half)], kq_buffer.at[t], sems.at[2 + t])
        for t, ref in enumerate((k_ref, q_ref))
    ]
    large.append(pltpu.make_async_copy(v_ref, v_buffer, sems.at[4]))
    for copy in small + large:
        copy.start()
    for copy in small:
        copy.wait()
    own_hot, _ = places(counts, cap)
    row, column = grid_of(cap)
    position = (index * TOK_DEV + pos[0:1, :]).astype(F32)
    position = jnp.sum(jnp.where(row == column, position, 0.0), axis=1, keepdims=True)
    lane = lax.broadcasted_iota(jnp.int32, (cap, HEAD_DIM), 1)
    feature = jnp.where(lane < HALF_DIM, lane, lane - HALF_DIM).astype(F32)
    angle = position * jnp.exp(feature * (-2.0 / HEAD_DIM * math.log(THETA)))
    table_ref[0] = jnp.cos(angle)
    table_ref[1] = jnp.where(lane < HALF_DIM, -1.0, 1.0) * jnp.sin(angle)
    for t in range(2):
        large[t].wait()
        for h in range(heads):
            out_ref[t, :, lanes(h)] = put(own_hot, rotated(kq_buffer[t, :, lanes(h)], table_ref, 1))
    large[2].wait()
    for m in range(groups):
        for side in range(2):
            block = (parity ^ side) * groups + (group ^ m)
            outs[m][side] = put(own_hot, v_buffer[:, lanes(block, wide)])


def gate_kernel(counts, weight_ref, input_ref, g_ref, out_ref, gate_ref):
    cap, half = out_ref.shape
    parity = own_place(counts)[0]
    own_hot, _ = places(counts, cap)
    total = jnp.zeros((cap, HEAD_DIM), F32)
    for b in range(input_ref.shape[1] // HEAD_DIM):
        total += input_ref[:, lanes(b)].astype(F32) * weight_ref[0:1, lanes(b)].astype(F32)
    logit = jnp.sum(total, axis=1, keepdims=True)
    gate = jnp.broadcast_to(1.0 / (1.0 + jnp.exp(-logit)), (cap, HEAD_DIM))
    gate_ref[...] = gate
    heads = half // HEAD_DIM
    for h in range(heads):
        rows = g_ref[:, lanes((1 - parity) * heads + h)].astype(F32) * gate
        out_ref[:, lanes(h)] = put(own_hot, rows.astype(BF16))


def pack_kernel(groups, counts, table_ref, k_ref, q_ref, in_ref, *outs):
    cap, half = in_ref.shape[1:]
    parity, group, _ = own_place(counts)
    own_hot, _ = places(counts, cap)
    heads = half // groups // HEAD_DIM
    for m in range(groups):
        for t, ref in enumerate((k_ref, q_ref)):
            for c in range(heads):
                h = (group ^ m) * heads + c
                rows = rotated(ref[:, lanes(parity * groups * heads + h)], table_ref, 1)
                outs[m][t, :, lanes(c)] = put(own_hot, rows) + in_ref[t, :, lanes(h)]


def pack_gated_kernel(groups, counts, gate_ref, g_ref, in_ref, *outs):
    cap, half = in_ref.shape
    parity, group, _ = own_place(counts)
    own_hot, _ = places(counts, cap)
    heads = half // groups // HEAD_DIM
    for m in range(groups):
        for c in range(heads):
            h = (group ^ m) * heads + c
            rows = g_ref[:, lanes(parity * groups * heads + h)].astype(F32) * gate_ref[...]
            outs[m][:, lanes(c)] = put(own_hot, rows.astype(BF16)) + in_ref[:, lanes(h)]


def block_of(m, cap):
    return pl.ds(pl.multiple_of(((lax.axis_index("seq") >> 1) ^ m) * cap, cap), cap)


def gather_values_kernel(groups, counts, *refs):
    own_ref, send_ref = refs[groups:]
    cap = refs[0].shape[1]
    for i in range(groups):
        block = block_of(groups - 1 - i, cap)
        own_ref[block, :] = refs[i][0]
        send_ref[block, :] = refs[i][1]


def gather_kernel(groups, counts, v_own_ref, v_in_ref, *refs):
    cap = refs[0].shape[1]
    for i in range(groups):
        refs[groups][0:2, block_of(groups - 1 - i, cap), :] = refs[i][...]
    refs[groups][2] = v_own_ref[...] + v_in_ref[...]


def probabilities_kernel(groups, counts, kqv_ref, *refs):
    g_refs, (dv_ref, ds_ref, delta_ref, g_ref, sum_ref) = refs[:groups], refs[groups:]
    total = ds_ref.shape[2]
    cap, wide = g_refs[0].shape
    for i in range(groups):
        g_ref[block_of(groups - 1 - i, cap), :] = g_refs[i][...]
    key, query = grid_of(cap)
    kept = query >= key
    for c in range(wide // HEAD_DIM):
        sum_ref[...] = jnp.zeros_like(sum_ref)
        for i in range(groups):
            upto = (i + 1) * cap
            here = slice(i * cap, upto)
            g = g_ref[here, lanes(c)]
            s = dot(kqv_ref[0, :upto, lanes(c)], kqv_ref[1, here, lanes(c)], ((1,), (1,))) * SCALE
            last = jnp.where(kept, s[i * cap:], NEG)
            s = last if i == 0 else jnp.concatenate([s[:i * cap], last], axis=0)
            e = jnp.exp(s - jnp.max(s, axis=0, keepdims=True))
            p = e * (1.0 / jnp.sum(e, axis=0, keepdims=True))
            dp = dot(kqv_ref[2, :upto, lanes(c)], g, ((1,), (1,)))
            delta = jnp.sum(p * dp, axis=0, keepdims=True)
            whole = jnp.broadcast_to(delta, (8, cap))
            delta_ref[i] = whole if c == 0 else delta_ref[i] + whole
            p16 = p.astype(BF16)
            ds_ref[c, i, :upto, :] = (p16.astype(F32) * (dp - delta) * SCALE).astype(BF16)
            sum_ref[:upto, :] += dot(p16, g, ((1,), (0,)))
        dv_ref[:total, lanes(c)] = sum_ref[...].astype(BF16)
    extra = dv_ref.shape[0] - total
    line = lax.broadcasted_iota(jnp.int32, (extra, cap), 0)
    rows = jnp.zeros((extra, cap), F32)
    for i in range(groups):
        delta = delta_ref[i][0:1, :]
        coarse = delta.astype(BF16).astype(F32)
        rows = jnp.where(line == 2 * i, coarse, jnp.where(line == 2 * i + 1, delta - coarse, rows))
    for c in range(wide // HEAD_DIM):
        dv_ref[total:, lanes(c)] = rows.astype(BF16)


def part_values_kernel(groups, counts, dv_ref, dv_in_ref, *outs):
    cap = outs[0].shape[1]
    for m in range(groups):
        block = block_of(m, cap)
        outs[m][0] = dv_ref[block, :]
        outs[m][1] = dv_in_ref[block, :]


def grad_keys_kernel(groups, counts, kqv_ref, ds_ref, *refs):
    outs, sum_ref = refs[:groups], refs[groups]
    heads, _, total, cap = ds_ref.shape
    for c in range(heads):
        sum_ref[...] = jnp.zeros_like(sum_ref)
        for i in range(groups):
            upto = (i + 1) * cap
            sum_ref[:upto, :] += dot(ds_ref[c, i, :upto, :], kqv_ref[1, i * cap:upto, lanes(c)], ((1,), (0,)))
        for m in range(groups):
            outs[m][:, lanes(c)] = sum_ref[block_of(m, cap), :].astype(BF16)


def grad_queries_kernel(groups, counts, kqv_ref, ds_ref, dv_ref, dv_in_ref, *refs):
    outs, sum_ref = refs[:groups], refs[groups]
    heads, _, total, cap = ds_ref.shape
    for c in range(heads):
        for i in range(groups):
            upto = (i + 1) * cap
            sum_ref[i * cap:upto, :] = dot(ds_ref[c, i, :upto, :], kqv_ref[0, :upto, lanes(c)], ((0,), (0,)))
        for m in range(groups):
            outs[m][0:cap, lanes(c)] = sum_ref[block_of(m, cap), :].astype(BF16)
    both = dv_ref[total:, 0:HEAD_DIM].astype(F32) + dv_in_ref[total:, 0:HEAD_DIM].astype(F32)
    line = lax.broadcasted_iota(jnp.int32, both.shape, 0)
    out_line = lax.broadcasted_iota(jnp.int32, (16, cap), 0)
    for m in range(groups):
        group = own_place(counts)[1] ^ m
        delta = jnp.sum(jnp.where((line >> 1) == group, both, 0.0), axis=0, keepdims=True)
        coarse = delta.astype(BF16).astype(F32)
        rows = jnp.where(out_line == 0, coarse, jnp.where(out_line == 1, delta - coarse, 0.0)).astype(BF16)
        for c in range(heads):
            outs[m][cap:, lanes(c)] = rows


def unpack_kernel(groups, counts, table_ref, *refs):
    ins, own_ref, send_ref, delta_ref = refs[:groups], refs[groups], refs[groups + 1], refs[groups + 2]
    cap = own_ref.shape[0]
    wide = ins[0].shape[1]
    heads = wide // HEAD_DIM
    own_hot, in_hot = places(counts, cap)
    delta = jnp.zeros((16, HEAD_DIM), F32)
    for i in range(groups):
        if ins[0].shape[0] > cap:
            delta += ins[i][cap:, 0:HEAD_DIM].astype(F32)
        group = own_place(counts)[1] ^ (groups - 1 - i)
        send_ref[:, lanes(group, wide)] = taken(in_hot, ins[i][0:cap, :])
        for c in range(heads):
            own = dot(own_hot, ins[i][0:cap, lanes(c)], ((0,), (0,)))
            own_ref[:, lanes(group * heads + c)] = rotated(own, table_ref, -1)
    delta_ref[...] = jnp.broadcast_to(delta[0:1, :] + delta[1:2, :], delta_ref.shape)


def router_kernel(counts, gate_ref, input_ref, *refs):
    deltas, out_ref = refs[:-1], refs[-1]
    cap = input_ref.shape[0]
    parity, _, count = own_place(counts)
    row, column = grid_of(cap)
    start = jnp.where(parity == 0, 0, cap - count)
    own = jnp.where((column == row + start) & (row < count), sum(ref[0:1, :] for ref in deltas), 0.0)
    term = (1.0 - gate_ref[...]) * jnp.sum(own, axis=1, keepdims=True)
    for b in range(out_ref.shape[0]):
        out_ref[b:b + 1, :] = jnp.sum(input_ref[:, lanes(b)].astype(F32) * term, axis=0, keepdims=True)


def total_kernel(in_ref, out_ref):
    out_ref[...] = jnp.sum(in_ref[...], axis=0, keepdims=True)


def place_values_kernel(groups, counts, *refs):
    ins, out_ref, token_ref = refs[:groups], refs[groups], refs[groups + 1]
    cap, wide = ins[0].shape[1:]
    parity, group, _ = own_place(counts)
    own_hot, _ = places(counts, cap)
    token_ref[...] = jnp.zeros_like(token_ref)
    for i in range(groups):
        for side in range(2):
            block = (parity ^ side) * groups + (group ^ (groups - 1 - i))
            out_ref[:, lanes(block, wide)] = taken(own_hot, ins[i][side])


def place_kernel(counts, table_ref, own_ref, in_ref, out_ref, token_ref):
    half = own_ref.shape[1]
    heads = half // HEAD_DIM
    parity = own_place(counts)[0]
    out_ref[:, lanes(parity, half)] = own_ref[...]
    token_ref[...] = jnp.zeros_like(token_ref)
    for h in range(heads):
        out_ref[:, lanes((1 - parity) * heads + h)] = rotated(in_ref[:, lanes(h)], table_ref, -1)


def per_device(queries, key_rows, value_rows, out_grad, inputs, router_weight, counts, picked_pos):
    query_own, key_own, value_own, grad_own, input_own = queries[0], key_rows[0], value_rows[0], out_grad[0], inputs[0]
    cap, width = query_own.shape
    half = width // 2
    seq_size = lax.axis_size("seq")
    groups = seq_size // 2
    wide = half // groups
    total = groups * cap
    heads = wide // HEAD_DIM

    def kernel(body):
        return functools.partial(body, groups)

    *values, sent, table = pl.pallas_call(
        kernel(front_kernel),
        in_specs=[SMEM] + [HBM] * 4,
        out_specs=[VMEM] * (groups + 2),
        out_shape=[jax.ShapeDtypeStruct((2, cap, wide), BF16)] * groups
        + [jax.ShapeDtypeStruct((2, cap, half), BF16), jax.ShapeDtypeStruct((2, cap, HEAD_DIM), F32)],
        scratch_shapes=[
            pltpu.VMEM((1, cap), jnp.int32),
            pltpu.VMEM((cap, width), BF16),
            pltpu.VMEM((2, cap, half), BF16),
            pltpu.SemaphoreType.DMA((5,)),
        ],
        compiler_params=pltpu.CompilerParams(vmem_limit_bytes=63 * 1024 * 1024),
        cost_estimate=cost("front"),
        name="front",
    )(counts, picked_pos, value_own, key_own, query_own)
    kq_in = swapped(sent)
    values = spread(values)
    router_full = lax.all_gather(router_weight, "fsdp", axis=0, tiled=True)
    sent, gate = call(
        gate_kernel, "gate", [((cap, half), BF16), ((cap, HEAD_DIM), F32)], counts, router_full[None, :], input_own, grad_own
    )
    g_in = swapped(sent)
    kq = spread(call(
        kernel(pack_kernel),
        "pack",
        [((2, cap, wide), BF16)] * groups,
        counts, table, key_own, query_own, kq_in,
    ))
    v_own, sent = call(
        kernel(gather_values_kernel), "gather_values", [((total, wide), BF16)] * 2, counts, *values, wait=kq[-1:]
    )
    v_in = swapped(sent)
    gated = spread(call(
        kernel(pack_gated_kernel),
        "pack_gated",
        [((cap, wide), BF16)] * groups,
        counts, gate, grad_own, g_in, wait=[v_own],
    ))
    kqv = call(
        kernel(gather_kernel), "gather", [((3, total, wide), BF16)], counts, v_own, v_in, *kq
    )[0]

    piece = ((cap, wide), BF16)
    extra = 16 * ((2 * groups + 15) // 16)
    dv, ds = call(
        kernel(probabilities_kernel),
        "probabilities",
        [((total + extra, wide), BF16), ((heads, groups, total, cap), BF16)],
        counts, kqv, *gated,
        scratch_shapes=[
            pltpu.VMEM((groups, 8, cap), F32), pltpu.VMEM((total, wide), BF16), pltpu.VMEM((total, HEAD_DIM), F32),
        ],
    )
    dv_in = swapped(dv)
    k_pieces = spread(call(
        kernel(grad_keys_kernel),
        "grad_keys",
        [piece] * groups,
        counts, kqv, ds,
        scratch_shapes=[pltpu.VMEM((total, HEAD_DIM), F32)],
    ))

    def unpacked(name, pieces, wait):
        shapes = [((cap, half), BF16)] * 2 + [((8, cap), F32)]
        return call(kernel(unpack_kernel), name, shapes, counts, table, *pieces, wait=wait)

    def placed(name, own, other, wait):
        return call(place_kernel, name, [((cap, width), BF16), ((8, HEAD_DIM), F32)], counts, table, own, other, wait=wait)

    q_pieces = spread(call(
        kernel(grad_queries_kernel),
        "grad_queries",
        [((cap + 16, wide), BF16)] * groups,
        counts, kqv, ds, dv, dv_in,
        wait=k_pieces[-1:],
        scratch_shapes=[pltpu.VMEM((total, HEAD_DIM), F32)],
    ))
    parts = call(
        kernel(part_values_kernel), "part_values", [((2, cap, wide), BF16)] * groups, counts, dv, dv_in, wait=q_pieces[-1:]
    )
    v_pieces = spread(parts)
    k_own, sent, token_k = unpacked("unpack_keys", k_pieces, parts[:1])
    k_in = swapped(sent)
    q_own, sent, delta = unpacked("unpack_queries", q_pieces, [token_k])
    q_in = swapped(sent)
    (part,) = call(
        router_kernel, "router", [((input_own.shape[1] // HEAD_DIM, HEAD_DIM), F32)], counts, gate, input_own, delta
    )
    shape = [((cap, width), BF16), ((8, HEAD_DIM), F32)]
    grad_v, token_v = call(kernel(place_values_kernel), "place_values", shape, counts, *v_pieces)
    grad_k, token_k = placed("place_keys", k_own, k_in, [token_v])
    grad_q, token_q = placed("place_queries", q_own, q_in, [token_k])
    devices = seq_size * lax.axis_size("fsdp")
    shares = lax.all_to_all(part.reshape(devices, -1), ("seq", "fsdp"), 0, 0, tiled=True)
    grad_router = call(total_kernel, "total", [((1, shares.shape[1]), F32)], shares, wait=[token_q])[0][0]
    return grad_q[None], grad_k[None], grad_v[None], grad_router


def solution(mesh):
    rows = P("fsdp", "seq", None)
    placed = (rows, rows, rows, rows, rows, P("fsdp"), P("fsdp", "seq"), P("fsdp", "seq"))
    return jax.shard_map(
        per_device,
        mesh=mesh,
        in_specs=placed,
        out_specs=(rows, rows, rows, P(("seq", "fsdp"))),
        check_vma=False,
    )
```

```python
import functools
import math

import jax
import jax.numpy as jnp
from jax import lax
from jax.experimental import pallas as pl
from jax.experimental.pallas import tpu as pltpu
from jax.sharding import PartitionSpec as P

HEADS = 16
HEAD_DIM = 128
HALF_DIM = HEAD_DIM // 2
TOK_DEV = 512
THETA = 500000.0
NEG = -1e30
SCALE = HEAD_DIM ** -0.5
BF16 = jnp.bfloat16
F32 = jnp.float32
PARAMS = pltpu.CompilerParams(vmem_limit_bytes=40 * 1024 * 1024)
COSTS = {"place_keys": 0.5, "router": 1}
VMEM = pl.BlockSpec(memory_space=pltpu.VMEM)
ANY = pl.BlockSpec(memory_space=pl.ANY)
HBM = pl.BlockSpec(memory_space=pltpu.HBM)
SMEM = pl.BlockSpec(memory_space=pltpu.SMEM)


def swapped(array):
    return lax.ppermute(array, "seq", [(i, i ^ 1) for i in range(lax.axis_size("seq"))])


def spread(pieces):
    size = lax.axis_size("seq")
    arrived = [
        lax.ppermute(pieces[m], "seq", [(i, i ^ (2 * m)) for i in range(size)]) for m in range(len(pieces) - 1, 0, -1)
    ]
    return arrived + [pieces[0]]


def cost(name):
    return pl.CostEstimate(flops=int(COSTS.get(name, 0.001) * 1e9), bytes_accessed=1 << 16, transcendentals=0)


def call(kernel, name, shapes, *operands, wait=(), scratch_shapes=()):
    count = len(operands)

    def body(*refs):
        kernel(*refs[:count], *refs[count + len(wait):])

    return pl.pallas_call(
        body,
        in_specs=[SMEM if a.shape == (1, 1) else VMEM for a in operands] + [ANY] * len(wait),
        out_specs=[VMEM] * len(shapes),
        out_shape=[jax.ShapeDtypeStruct(shape, dtype) for shape, dtype in shapes],
        scratch_shapes=scratch_shapes,
        compiler_params=PARAMS,
        cost_estimate=cost(name),
        name=name,
    )(*operands, *wait)


def dot(a, b, contract):
    return lax.dot_general(a, b, ((contract[0], contract[1]), ((), ())), preferred_element_type=F32)


def lanes(index, width=HEAD_DIM):
    if isinstance(index, int):
        return slice(index * width, (index + 1) * width)
    return pl.ds(pl.multiple_of(index * width, HEAD_DIM), width)


def grid_of(cap):
    row = lax.broadcasted_iota(jnp.int32, (cap, cap), 0)
    column = lax.broadcasted_iota(jnp.int32, (cap, cap), 1)
    return row, column


def own_place(counts):
    index = lax.axis_index("seq")
    return index & 1, index >> 1, counts[0, 0]


def places(counts, cap):
    parity, _, count = own_place(counts)
    first = jnp.where(parity == 0, count, cap - count)
    row, slot = grid_of(cap)
    even = jnp.where((row == slot) & (row < first), 1.0, 0.0)
    odd = jnp.where((row == slot + first) & (row >= first), 1.0, 0.0)
    is_even = parity == 0
    return jnp.where(is_even, even, odd).astype(BF16), jnp.where(is_even, odd, even).astype(BF16)


def rotated(rows, table_ref, direction):
    rows = rows.astype(F32)
    turned = pltpu.roll(rows, HALF_DIM, 1) * table_ref[1]
    rows = rows * table_ref[0]
    return (rows + turned if direction > 0 else rows - turned).astype(BF16)


def put(hot, rows):
    return dot(hot, rows, ((1,), (0,))).astype(BF16)


def taken(hot, rows):
    return dot(hot, rows, ((0,), (0,))).astype(BF16)


def front_kernel(groups, counts, pos_ref, v_ref, k_ref, q_ref, *refs):
    outs, out_ref, table_ref = refs[:groups], refs[groups], refs[groups + 1]
    pos, v_buffer, kq_buffer, sems = refs[groups + 2:]
    cap, half = out_ref.shape[1:]
    wide = outs[0].shape[2]
    heads = half // HEAD_DIM
    index = lax.axis_index("seq")
    parity, group = index & 1, index >> 1
    small = [pltpu.make_async_copy(pos_ref, pos, sems.at[1])]
    large = [
        pltpu.make_async_copy(ref.at[:, lanes(1 - parity, half)], kq_buffer.at[t], sems.at[2 + t])
        for t, ref in enumerate((k_ref, q_ref))
    ]
    large.append(pltpu.make_async_copy(v_ref, v_buffer, sems.at[4]))
    for copy in small + large:
        copy.start()
    for copy in small:
        copy.wait()
    own_hot, _ = places(counts, cap)
    row, column = grid_of(cap)
    position = (index * TOK_DEV + pos[0:1, :]).astype(F32)
    position = jnp.sum(jnp.where(row == column, position, 0.0), axis=1, keepdims=True)
    lane = lax.broadcasted_iota(jnp.int32, (cap, HEAD_DIM), 1)
    feature = jnp.where(lane < HALF_DIM, lane, lane - HALF_DIM).astype(F32)
    angle = position * jnp.exp(feature * (-2.0 / HEAD_DIM * math.log(THETA)))
    table_ref[0] = jnp.cos(angle)
    table_ref[1] = jnp.where(lane < HALF_DIM, -1.0, 1.0) * jnp.sin(angle)
    for t in range(2):
        large[t].wait()
        for h in range(heads):
            out_ref[t, :, lanes(h)] = put(own_hot, rotated(kq_buffer[t, :, lanes(h)], table_ref, 1))
    large[2].wait()
    for m in range(groups):
        for side in range(2):
            block = (parity ^ side) * groups + (group ^ m)
            outs[m][side] = put(own_hot, v_buffer[:, lanes(block, wide)])


def gate_kernel(counts, weight_ref, input_ref, g_ref, out_ref, gate_ref):
    cap, half = out_ref.shape
    parity = own_place(counts)[0]
    own_hot, _ = places(counts, cap)
    total = jnp.zeros((cap, HEAD_DIM), F32)
    for b in range(input_ref.shape[1] // HEAD_DIM):
        total += input_ref[:, lanes(b)].astype(F32) * weight_ref[0:1, lanes(b)].astype(F32)
    logit = jnp.sum(total, axis=1, keepdims=True)
    gate = jnp.broadcast_to(1.0 / (1.0 + jnp.exp(-logit)), (cap, HEAD_DIM))
    gate_ref[...] = gate
    heads = half // HEAD_DIM
    for h in range(heads):
        rows = g_ref[:, lanes((1 - parity) * heads + h)].astype(F32) * gate
        out_ref[:, lanes(h)] = put(own_hot, rows.astype(BF16))


def pack_kernel(groups, counts, table_ref, k_ref, q_ref, in_ref, *outs):
    cap, half = in_ref.shape[1:]
    parity, group, _ = own_place(counts)
    own_hot, _ = places(counts, cap)
    heads = half // groups // HEAD_DIM
    for m in range(groups):
        for t, ref in enumerate((k_ref, q_ref)):
            for c in range(heads):
                h = (group ^ m) * heads + c
                rows = rotated(ref[:, lanes(parity * groups * heads + h)], table_ref, 1)
                outs[m][t, :, lanes(c)] = put(own_hot, rows) + in_ref[t, :, lanes(h)]


def pack_gated_kernel(groups, counts, gate_ref, g_ref, in_ref, *outs):
    cap, half = in_ref.shape
    parity, group, _ = own_place(counts)
    own_hot, _ = places(counts, cap)
    heads = half // groups // HEAD_DIM
    for m in range(groups):
        for c in range(heads):
            h = (group ^ m) * heads + c
            rows = g_ref[:, lanes(parity * groups * heads + h)].astype(F32) * gate_ref[...]
            outs[m][:, lanes(c)] = put(own_hot, rows.astype(BF16)) + in_ref[:, lanes(h)]


def block_of(m, cap):
    return pl.ds(pl.multiple_of(((lax.axis_index("seq") >> 1) ^ m) * cap, cap), cap)


def gather_values_kernel(groups, counts, *refs):
    own_ref, send_ref = refs[groups:]
    cap = refs[0].shape[1]
    for i in range(groups):
        block = block_of(groups - 1 - i, cap)
        own_ref[block, :] = refs[i][0]
        send_ref[block, :] = refs[i][1]


def gather_kernel(groups, counts, v_own_ref, v_in_ref, *refs):
    cap = refs[0].shape[1]
    for i in range(groups):
        refs[groups][0:2, block_of(groups - 1 - i, cap), :] = refs[i][...]
    refs[groups][2] = v_own_ref[...] + v_in_ref[...]


def probabilities_kernel(groups, counts, kqv_ref, *refs):
    g_refs, (dv_ref, ds_ref, delta_ref, g_ref, sum_ref) = refs[:groups], refs[groups:]
    total = ds_ref.shape[2]
    cap, wide = g_refs[0].shape
    for i in range(groups):
        g_ref[block_of(groups - 1 - i, cap), :] = g_refs[i][...]
    key, query = grid_of(cap)
    kept = query >= key
    for c in range(wide // HEAD_DIM):
        sum_ref[...] = jnp.zeros_like(sum_ref)
        for i in range(groups):
            upto = (i + 1) * cap
            here = slice(i * cap, upto)
            g = g_ref[here, lanes(c)]
            s = dot(kqv_ref[0, :upto, lanes(c)], kqv_ref[1, here, lanes(c)], ((1,), (1,))) * SCALE
            last = jnp.where(kept, s[i * cap:], NEG)
            s = last if i == 0 else jnp.concatenate([s[:i * cap], last], axis=0)
            e = jnp.exp(s - jnp.max(s, axis=0, keepdims=True))
            p = e * (1.0 / jnp.sum(e, axis=0, keepdims=True))
            dp = dot(kqv_ref[2, :upto, lanes(c)], g, ((1,), (1,)))
            delta = jnp.sum(p * dp, axis=0, keepdims=True)
            whole = jnp.broadcast_to(delta, (8, cap))
            delta_ref[i] = whole if c == 0 else delta_ref[i] + whole
            p16 = p.astype(BF16)
            ds_ref[c, i, :upto, :] = (p16.astype(F32) * (dp - delta) * SCALE).astype(BF16)
            sum_ref[:upto, :] += dot(p16, g, ((1,), (0,)))
        dv_ref[:total, lanes(c)] = sum_ref[...].astype(BF16)
    extra = dv_ref.shape[0] - total
    line = lax.broadcasted_iota(jnp.int32, (extra, cap), 0)
    rows = jnp.zeros((extra, cap), F32)
    for i in range(groups):
        delta = delta_ref[i][0:1, :]
        coarse = delta.astype(BF16).astype(F32)
        rows = jnp.where(line == 2 * i, coarse, jnp.where(line == 2 * i + 1, delta - coarse, rows))
    for c in range(wide // HEAD_DIM):
        dv_ref[total:, lanes(c)] = rows.astype(BF16)


def part_values_kernel(groups, counts, dv_ref, dv_in_ref, *outs):
    cap = outs[0].shape[1]
    for m in range(groups):
        block = block_of(m, cap)
        outs[m][0] = dv_ref[block, :]
        outs[m][1] = dv_in_ref[block, :]


def grad_keys_kernel(groups, counts, kqv_ref, ds_ref, *refs):
    outs, sum_ref = refs[:groups], refs[groups]
    heads, _, total, cap = ds_ref.shape
    for c in range(heads):
        sum_ref[...] = jnp.zeros_like(sum_ref)
        for i in range(groups):
            upto = (i + 1) * cap
            sum_ref[:upto, :] += dot(ds_ref[c, i, :upto, :], kqv_ref[1, i * cap:upto, lanes(c)], ((1,), (0,)))
        for m in range(groups):
            outs[m][:, lanes(c)] = sum_ref[block_of(m, cap), :].astype(BF16)


def grad_queries_kernel(groups, counts, kqv_ref, ds_ref, dv_ref, dv_in_ref, *refs):
    outs, sum_ref = refs[:groups], refs[groups]
    heads, _, total, cap = ds_ref.shape
    for c in range(heads):
        for i in range(groups):
            upto = (i + 1) * cap
            sum_ref[i * cap:upto, :] = dot(ds_ref[c, i, :upto, :], kqv_ref[0, :upto, lanes(c)], ((0,), (0,)))
        for m in range(groups):
            outs[m][0:cap, lanes(c)] = sum_ref[block_of(m, cap), :].astype(BF16)
    both = dv_ref[total:, 0:HEAD_DIM].astype(F32) + dv_in_ref[total:, 0:HEAD_DIM].astype(F32)
    line = lax.broadcasted_iota(jnp.int32, both.shape, 0)
    out_line = lax.broadcasted_iota(jnp.int32, (16, cap), 0)
    for m in range(groups):
        group = own_place(counts)[1] ^ m
        delta = jnp.sum(jnp.where((line >> 1) == group, both, 0.0), axis=0, keepdims=True)
        coarse = delta.astype(BF16).astype(F32)
        rows = jnp.where(out_line == 0, coarse, jnp.where(out_line == 1, delta - coarse, 0.0)).astype(BF16)
        for c in range(heads):
            outs[m][cap:, lanes(c)] = rows


def unpack_kernel(groups, counts, table_ref, *refs):
    ins, own_ref, send_ref, delta_ref = refs[:groups], refs[groups], refs[groups + 1], refs[groups + 2]
    cap = own_ref.shape[0]
    wide = ins[0].shape[1]
    heads = wide // HEAD_DIM
    own_hot, in_hot = places(counts, cap)
    delta = jnp.zeros((16, HEAD_DIM), F32)
    for i in range(groups):
        if ins[0].shape[0] > cap:
            delta += ins[i][cap:, 0:HEAD_DIM].astype(F32)
        group = own_place(counts)[1] ^ (groups - 1 - i)
        send_ref[:, lanes(group, wide)] = taken(in_hot, ins[i][0:cap, :])
        for c in range(heads):
            own = dot(own_hot, ins[i][0:cap, lanes(c)], ((0,), (0,)))
            own_ref[:, lanes(group * heads + c)] = rotated(own, table_ref, -1)
    delta_ref[...] = jnp.broadcast_to(delta[0:1, :] + delta[1:2, :], delta_ref.shape)


def router_kernel(counts, gate_ref, input_ref, *refs):
    deltas, out_ref = refs[:-1], refs[-1]
    cap = input_ref.shape[0]
    parity, _, count = own_place(counts)
    row, column = grid_of(cap)
    start = jnp.where(parity == 0, 0, cap - count)
    own = jnp.where((column == row + start) & (row < count), sum(ref[0:1, :] for ref in deltas), 0.0)
    term = (1.0 - gate_ref[...]) * jnp.sum(own, axis=1, keepdims=True)
    for b in range(out_ref.shape[0]):
        out_ref[b:b + 1, :] = jnp.sum(input_ref[:, lanes(b)].astype(F32) * term, axis=0, keepdims=True)


def total_kernel(in_ref, out_ref):
    out_ref[...] = jnp.sum(in_ref[...], axis=0, keepdims=True)


def place_values_kernel(groups, counts, *refs):
    ins, out_ref, token_ref = refs[:groups], refs[groups], refs[groups + 1]
    cap, wide = ins[0].shape[1:]
    parity, group, _ = own_place(counts)
    own_hot, _ = places(counts, cap)
    token_ref[...] = jnp.zeros_like(token_ref)
    for i in range(groups):
        for side in range(2):
            block = (parity ^ side) * groups + (group ^ (groups - 1 - i))
            out_ref[:, lanes(block, wide)] = taken(own_hot, ins[i][side])


def place_kernel(counts, table_ref, own_ref, in_ref, out_ref, token_ref):
    half = own_ref.shape[1]
    heads = half // HEAD_DIM
    parity = own_place(counts)[0]
    out_ref[:, lanes(parity, half)] = own_ref[...]
    token_ref[...] = jnp.zeros_like(token_ref)
    for h in range(heads):
        out_ref[:, lanes((1 - parity) * heads + h)] = rotated(in_ref[:, lanes(h)], table_ref, -1)


def per_device(queries, key_rows, value_rows, out_grad, inputs, router_weight, counts, picked_pos):
    query_own, key_own, value_own, grad_own, input_own = queries[0], key_rows[0], value_rows[0], out_grad[0], inputs[0]
    cap, width = query_own.shape
    half = width // 2
    seq_size = lax.axis_size("seq")
    groups = seq_size // 2
    wide = half // groups
    total = groups * cap
    heads = wide // HEAD_DIM

    def kernel(body):
        return functools.partial(body, groups)

    *values, sent, table = pl.pallas_call(
        kernel(front_kernel),
        in_specs=[SMEM] + [HBM] * 4,
        out_specs=[VMEM] * (groups + 2),
        out_shape=[jax.ShapeDtypeStruct((2, cap, wide), BF16)] * groups
        + [jax.ShapeDtypeStruct((2, cap, half), BF16), jax.ShapeDtypeStruct((2, cap, HEAD_DIM), F32)],
        scratch_shapes=[
            pltpu.VMEM((1, cap), jnp.int32),
            pltpu.VMEM((cap, width), BF16),
            pltpu.VMEM((2, cap, half), BF16),
            pltpu.SemaphoreType.DMA((5,)),
        ],
        compiler_params=pltpu.CompilerParams(vmem_limit_bytes=63 * 1024 * 1024),
        cost_estimate=cost("front"),
        name="front",
    )(counts, picked_pos, value_own, key_own, query_own)
    kq_in = swapped(sent)
    values = spread(values)
    router_full = lax.all_gather(router_weight, "fsdp", axis=0, tiled=True)
    sent, gate = call(
        gate_kernel, "gate", [((cap, half), BF16), ((cap, HEAD_DIM), F32)], counts, router_full[None, :], input_own, grad_own
    )
    g_in = swapped(sent)
    kq = spread(call(
        kernel(pack_kernel),
        "pack",
        [((2, cap, wide), BF16)] * groups,
        counts, table, key_own, query_own, kq_in,
    ))
    v_own, sent = call(
        kernel(gather_values_kernel), "gather_values", [((total, wide), BF16)] * 2, counts, *values
    )
    v_in = swapped(sent)
    gated = spread(call(
        kernel(pack_gated_kernel),
        "pack_gated",
        [((cap, wide), BF16)] * groups,
        counts, gate, grad_own, g_in, wait=[v_own],
    ))
    kqv = call(
        kernel(gather_kernel), "gather", [((3, total, wide), BF16)], counts, v_own, v_in, *kq
    )[0]

    piece = ((cap, wide), BF16)
    extra = 16 * ((2 * groups + 15) // 16)
    dv, ds = call(
        kernel(probabilities_kernel),
        "probabilities",
        [((total + extra, wide), BF16), ((heads, groups, total, cap), BF16)],
        counts, kqv, *gated,
        scratch_shapes=[
            pltpu.VMEM((groups, 8, cap), F32), pltpu.VMEM((total, wide), BF16), pltpu.VMEM((total, HEAD_DIM), F32),
        ],
    )
    dv_in = swapped(dv)
    k_pieces = spread(call(
        kernel(grad_keys_kernel),
        "grad_keys",
        [piece] * groups,
        counts, kqv, ds,
        scratch_shapes=[pltpu.VMEM((total, HEAD_DIM), F32)],
    ))

    def unpacked(name, pieces, wait):
        shapes = [((cap, half), BF16)] * 2 + [((8, cap), F32)]
        return call(kernel(unpack_kernel), name, shapes, counts, table, *pieces, wait=wait)

    def placed(name, own, other, wait):
        return call(place_kernel, name, [((cap, width), BF16), ((8, HEAD_DIM), F32)], counts, table, own, other, wait=wait)

    q_pieces = spread(call(
        kernel(grad_queries_kernel),
        "grad_queries",
        [((cap + 16, wide), BF16)] * groups,
        counts, kqv, ds, dv, dv_in,
        wait=k_pieces[-1:],
        scratch_shapes=[pltpu.VMEM((total, HEAD_DIM), F32)],
    ))
    parts = call(
        kernel(part_values_kernel), "part_values", [((2, cap, wide), BF16)] * groups, counts, dv, dv_in, wait=q_pieces[-1:]
    )
    v_pieces = spread(parts)
    k_own, sent, token_k = unpacked("unpack_keys", k_pieces, parts[:1])
    k_in = swapped(sent)
    q_own, sent, delta = unpacked("unpack_queries", q_pieces, [token_k])
    q_in = swapped(sent)
    (part,) = call(
        router_kernel, "router", [((input_own.shape[1] // HEAD_DIM, HEAD_DIM), F32)], counts, gate, input_own, delta
    )
    shape = [((cap, width), BF16), ((8, HEAD_DIM), F32)]
    grad_v, token_v = call(kernel(place_values_kernel), "place_values", shape, counts, *v_pieces)
    grad_k, token_k = placed("place_keys", k_own, k_in, [token_v])
    grad_q, token_q = placed("place_queries", q_own, q_in, [token_k])
    devices = seq_size * lax.axis_size("fsdp")
    shares = lax.all_to_all(part.reshape(devices, -1), ("seq", "fsdp"), 0, 0, tiled=True)
    grad_router = call(total_kernel, "total", [((1, shares.shape[1]), F32)], shares, wait=[token_q])[0][0]
    return grad_q[None], grad_k[None], grad_v[None], grad_router


def solution(mesh):
    rows = P("fsdp", "seq", None)
    placed = (rows, rows, rows, rows, rows, P("fsdp"), P("fsdp", "seq"), P("fsdp", "seq"))
    return jax.shard_map(
        per_device,
        mesh=mesh,
        in_specs=placed,
        out_specs=(rows, rows, rows, P(("seq", "fsdp"))),
        check_vma=False,
    )
```
